32 devices in a mesh: pp: 2 (over x), ep: 16 (over z, y, core).
Axes of the slice: x: 2, y: 2, z: 4, core: 2. Of those that a mesh axis runs over, the one named last changes fastest.
Arguments:
- fwd_act: bfloat16 [2, 1024, 3584], P('pp', 'ep'), may hold values from -6 to 6
- fwd_route: int32 [2, 1024, 1], P('pp', 'ep'), may hold values from 0 to 1, as said below
- fwd_gate: float32 [2, 1024, 1], P('pp', 'ep'), may hold values from 0.25 to 2
- bwd_act: bfloat16 [2, 1024, 3584], P('pp', 'ep'), may hold values from -6 to 6
- bwd_grad: bfloat16 [2, 1024, 3584], P('pp', 'ep'), may hold values from -6 to 6
- bwd_route: int32 [2, 1024, 1], P('pp', 'ep'), may hold values from 0 to 1, as said below
- bwd_gate: float32 [2, 1024, 1], P('pp', 'ep'), may hold values from 0.25 to 2
- norm_gain: float32 [2, 3584], P('pp'), may hold values from 0.25 to 1.75
- w_gate: bfloat16 [2, 16, 1792, 256], P('pp', 'ep'), may hold values from -0.09375 to 0.09375
- w_up: bfloat16 [2, 16, 1792, 256], P('pp', 'ep'), may hold values from -0.09375 to 0.09375
- w_down: bfloat16 [2, 16, 256, 1792], P('pp', 'ep'), may hold values from -0.1875 to 0.1875
Outputs:
- fwd_next: bfloat16 [2, 1024, 3584], P('pp', 'ep')
- bwd_next: bfloat16 [2, 1024, 3584], P('pp', 'ep')
The draws below stay inside these ranges and needn't reach their ends.
Inputs may be any that keep to these rules, and one draw needn't show every extreme that they name: `fwd_route`: among the 64 rows of one device, no expert is named more than 40 times; at each section one expert is named exactly 40 times in every device's rows. `bwd_route`: as fwd_route, drawn independently.
All inputs are finite; a program needn't handle non-finite values.
Results may differ from the reference program's by a relative error of at most 0.011.
Values may be sent and summed in bfloat16 or wider, within the bound.
No kernel may reach another device: no remote copies, remote signals or barrier semaphores. Data moves between devices by JAX's collectives and lax.ppermute only.
A program may use at most 128 MiB of HBM per device.

```python
import math
import jax
import jax.numpy as jnp
from jax import lax

D = 3584
H = 1024
SLICES = 8
TOPK = 1
TA = 64
EXPERTS = 2
HB = 256
CAP = 40
TOK = 1024
N_PP = 2
N_EP = 16


def route_helper(key, salt):
    mixed = jax.random.fold_in(key, salt)
    section_key, device_key = jax.random.split(mixed)
    favoured = jax.random.randint(section_key, (N_PP,), 0, EXPERTS, dtype=jnp.int32)

    def one_device(device_rand, chosen):
        label_key, order_key = jax.random.split(device_rand)
        labels = jnp.arange((EXPERTS - 1) * CAP, dtype=jnp.int32) // CAP
        labels = jax.random.permutation(label_key, labels)[:TA - CAP]
        labels = labels + (labels >= chosen).astype(jnp.int32)
        merged = jnp.concatenate([jnp.full((CAP,), chosen, dtype=jnp.int32), labels])
        return jax.random.permutation(order_key, merged)
    device_keys = jax.random.split(device_key, N_PP * N_EP)
    chosen_all = jnp.repeat(favoured, N_EP)
    routes = jax.vmap(one_device)(device_keys, chosen_all)
    return routes.reshape(N_PP, TOK, TOPK).astype(jnp.int32)


def draw_fwd_route(key, part):
    return route_helper(key, 11)


def draw_bwd_route(key, part):
    return route_helper(key, 23)


def block_scale(key, shape, cuts, low, high):
    loudness, own = 1.0, jax.random.fold_in(key, 6)
    for dim, shards_of in cuts:
        draws = jnp.exp(jax.random.uniform(jax.random.fold_in(own, dim), (shards_of,), jnp.float32, low / len(cuts), high / len(cuts)))
        loudness = loudness * jnp.repeat(draws, shape[dim] // shards_of).reshape([-1 if axis == dim else 1 for axis in range(len(shape))])
    return loudness


def gaussian(rng, dims, width, reach, shards=(), kind=jnp.bfloat16):
    gain = block_scale(rng, dims, shards, -0.22, 0.18) if shards else 1.0
    entries = jax.random.normal(rng, dims, jnp.float32) * width * gain
    return jnp.minimum(jnp.maximum(entries, -reach), reach).astype(kind)


def setup_inputs(seed: int = 0) -> dict:
    arg_keys = jax.random.split(jax.random.key(seed), 12)
    fwd_act = gaussian(arg_keys[0], (N_PP, TOK, D), 1.0, 6.0, ((0, 2), (1, 16)))
    fwd_route = draw_fwd_route(jax.random.fold_in(arg_keys[11], 71), 0)
    fwd_gate = jnp.clip(jnp.exp(math.log(2.0) - 2.0794415 * jax.random.uniform(arg_keys[2], (N_PP, TOK, TOPK), jnp.float32) ** block_scale(arg_keys[2], (N_PP, TOK, TOPK), ((0, 2), (1, 16)), -0.2, 0.2)), 0.25, 2.0)
    bwd_act = gaussian(arg_keys[3], (N_PP, TOK, D), 1.0, 6.0, ((0, 2), (1, 16)))
    bwd_grad = gaussian(arg_keys[4], (N_PP, TOK, D), 1.0, 6.0, ((0, 2), (1, 16)))
    bwd_route = draw_bwd_route(jax.random.fold_in(arg_keys[11], 71), 0)
    bwd_gate = jnp.clip(jnp.exp(math.log(2.0) - 2.0794415 * jax.random.uniform(arg_keys[6], (N_PP, TOK, TOPK), jnp.float32) ** block_scale(arg_keys[6], (N_PP, TOK, TOPK), ((0, 2), (1, 16)), -0.2, 0.2)), 0.25, 2.0)
    norm_gain = jnp.clip(1.0 + 0.15 * jax.random.normal(arg_keys[7], (N_PP, D), jnp.float32), 0.25, 1.75)
    w_gate = gaussian(arg_keys[8], (N_PP, N_EP, D // 2, HB), D ** -0.5, 0.09375, ((0, 2), (1, 16)))
    w_up = gaussian(arg_keys[9], (N_PP, N_EP, D // 2, HB), D ** -0.5, 0.09375, ((0, 2), (1, 16)))
    w_down = gaussian(arg_keys[10], (N_PP, N_EP, HB, D // 2), H ** -0.5, 0.1875, ((0, 2), (1, 16)))
    return {"fwd_act": fwd_act, "fwd_route": fwd_route, "fwd_gate": fwd_gate, "bwd_act": bwd_act, "bwd_grad": bwd_grad, "bwd_route": bwd_route, "bwd_gate": bwd_gate, "norm_gain": norm_gain, "w_gate": w_gate, "w_up": w_up, "w_down": w_down}


def normalize(values, norm_scale):
    widened = values.astype(jnp.float32)
    inverse = lax.rsqrt(lax.optimization_barrier(jnp.mean(widened * widened, axis=-1, keepdims=True)) + 1e-06)
    return ((widened * inverse * norm_scale).astype(jnp.bfloat16), inverse)

def build_slots(route_ids):
    by_source = route_ids.reshape(N_EP, TA)
    onehot = (by_source[:, :, None] == jnp.arange(EXPERTS, dtype=jnp.int32)[None, None, :]).astype(jnp.int32)
    running = jnp.cumsum(onehot, axis=1) - 1
    position = lax.optimization_barrier(jnp.sum(running * onehot, axis=2))
    sources = jnp.arange(N_EP, dtype=jnp.int32)[:, None]
    return (by_source * (N_EP * CAP) + sources * CAP + position).reshape(TOK).astype(jnp.int32)

def scatter_rows(values, target):
    buffer = jnp.zeros((EXPERTS * N_EP * CAP, D), values.dtype).at[target].set(values)
    return buffer.reshape(EXPERTS, N_EP * CAP, 2, D // 2)

def expert_forward(pieces):
    slots, gate_mat, up_mat, down_mat = pieces
    widened = slots.astype(jnp.float32)
    gate_pre = jnp.einsum('rkd,jkdf->rjf', widened, gate_mat.astype(jnp.float32))
    up_pre = jnp.einsum('rkd,jkdf->rjf', widened, up_mat.astype(jnp.float32))
    hidden = (jax.nn.silu(gate_pre) * up_pre).astype(jnp.bfloat16)
    partial_out = jnp.einsum('rjf,jkfd->rjkd', hidden.astype(jnp.float32), down_mat.astype(jnp.float32)).astype(jnp.bfloat16)
    return lax.optimization_barrier(jnp.sum(partial_out.astype(jnp.float32), axis=1))

def expert_backward(pieces):
    slots, grad_slots, gate_mat, up_mat, down_mat = pieces
    widened = slots.astype(jnp.float32)
    gate_f = gate_mat.astype(jnp.float32)
    up_f = up_mat.astype(jnp.float32)
    gate_pre = jnp.einsum('rkd,jkdf->rjf', widened, gate_f)
    up_pre = jnp.einsum('rkd,jkdf->rjf', widened, up_f)
    grad_hidden = jnp.einsum('rkd,jkfd->rjf', grad_slots.astype(jnp.float32), down_mat.astype(jnp.float32))
    logistic = jax.nn.sigmoid(gate_pre)
    d_gate = (grad_hidden * up_pre * logistic * (1.0 + gate_pre * (1.0 - logistic))).astype(jnp.bfloat16)
    d_up = (grad_hidden * gate_pre * logistic).astype(jnp.bfloat16)
    partial_in = (jnp.einsum('rjf,jkdf->rjkd', d_gate.astype(jnp.float32), gate_f) + jnp.einsum('rjf,jkdf->rjkd', d_up.astype(jnp.float32), up_f)).astype(jnp.bfloat16)
    return lax.optimization_barrier(jnp.sum(partial_in.astype(jnp.float32), axis=1))

def one_section(pieces):
    fwd_rows, fwd_ids, fwd_weight, bwd_rows, bwd_grads, bwd_ids, bwd_weight, norm_scale, gate_blocks, up_blocks, down_blocks = pieces
    gate_mats = gate_blocks.reshape(EXPERTS, SLICES // 2, 2, D // 2, HB)
    up_mats = up_blocks.reshape(EXPERTS, SLICES // 2, 2, D // 2, HB)
    down_mats = down_blocks.reshape(EXPERTS, SLICES // 2, 2, HB, D // 2)
    fwd_normed, fwd_inverse = normalize(fwd_rows, norm_scale)
    fwd_target = build_slots(fwd_ids[:, 0])
    fwd_slots = scatter_rows(fwd_normed, fwd_target)
    fwd_out = lax.map(expert_forward, (fwd_slots, gate_mats, up_mats, down_mats))
    fwd_mixed = fwd_out.reshape(EXPERTS * N_EP * CAP, D)[fwd_target]
    fwd_result = (fwd_rows.astype(jnp.float32) + fwd_weight * fwd_mixed).astype(jnp.bfloat16)
    bwd_normed, bwd_inverse = normalize(bwd_rows, norm_scale)
    weighted = (bwd_weight * bwd_grads.astype(jnp.float32)).astype(jnp.bfloat16)
    bwd_target = build_slots(bwd_ids[:, 0])
    bwd_slots = scatter_rows(bwd_normed, bwd_target)
    grad_slots = scatter_rows(weighted, bwd_target)
    bwd_out = lax.map(expert_backward, (bwd_slots, grad_slots, gate_mats, up_mats, down_mats))
    d_normed = bwd_out.reshape(EXPERTS * N_EP * CAP, D)[bwd_target]
    scaled = norm_scale * d_normed
    widened = bwd_rows.astype(jnp.float32)
    cubed = bwd_inverse * bwd_inverse * bwd_inverse
    d_rows = bwd_grads.astype(jnp.float32) + scaled * bwd_inverse - widened * cubed * lax.optimization_barrier(jnp.mean(scaled * widened, axis=-1, keepdims=True))
    return (fwd_result, d_rows.astype(jnp.bfloat16))

def reference(fwd_act, fwd_route, fwd_gate, bwd_act, bwd_grad, bwd_route, bwd_gate, norm_gain, w_gate, w_up, w_down):
    fwd_all, bwd_all = lax.map(one_section, (fwd_act, fwd_route, fwd_gate, bwd_act, bwd_grad, bwd_route, bwd_gate, norm_gain, w_gate, w_up, w_down))
    return (jnp.roll(fwd_all, 1, axis=0), jnp.roll(bwd_all, -1, axis=0))
```

```python
import jax
import jax.numpy as jnp
from jax import lax
from jax.sharding import PartitionSpec as P

SLICES = 8
NEAR, SIDE, FAR = 1, 2, 4


def swap(value, bit):
    return lax.ppermute(value, "ep", [(i, i ^ bit) for i in range(lax.axis_size("ep"))])


def to_expert(value, shift):
    count = lax.axis_size("ep")
    return lax.ppermute(value, "ep", [(i, (i + SLICES * shift) % count) for i in range(count)])


def to_section(value, step, place=lambda i: i):
    sections, count = lax.axis_size("pp"), lax.axis_size("ep")
    pairs = [
        (p * count + i, (p + step) % sections * count + place(i) % count)
        for p in range(sections)
        for i in range(count)
    ]
    return lax.ppermute(value, ("pp", "ep"), pairs)


def dot(a, b):
    return jnp.dot(a, b, preferred_element_type=jnp.float32)


def dot_t(a, b):
    return lax.dot_general(a, b, (((1,), (1,)), ((), ())), preferred_element_type=jnp.float32)


def inverse_rms(widened):
    return lax.rsqrt(jnp.mean(widened * widened, axis=-1, keepdims=True) + 1e-06)


def own_half_first(rows):
    half = rows.shape[1] // 2
    turned = jnp.concatenate([rows[:, half:], rows[:, :half]], axis=1)
    return jnp.where(lax.axis_index("ep") % 2 == 0, rows, turned)


def slot_plan(route_ids, experts, capacity):
    chosen = route_ids[:, 0]
    onehot = (chosen[:, None] == jnp.arange(experts, dtype=jnp.int32)[None, :]).astype(jnp.int32)
    position = jnp.sum((jnp.cumsum(onehot, axis=0) - 1) * onehot, axis=1)
    relative = (chosen - lax.axis_index("ep") // SLICES) % experts
    target = relative * capacity + position
    return target[:, None] == jnp.arange(experts * capacity, dtype=jnp.int32)[None, :]


def place(plan, shift, capacity, values):
    chooser = plan[:, shift * capacity : (shift + 1) * capacity].astype(jnp.bfloat16)
    return lax.dot_general(
        chooser, values, (((0,), (0,)), ((), ())), preferred_element_type=jnp.float32
    ).astype(jnp.bfloat16)


def spread(groups):
    mine = [groups[0]] + [to_expert(groups[r], r) for r in range(1, len(groups))]
    theirs = [swap(part, FAR) for part in mine]
    return mine + theirs


def send_back(partial, experts, capacity, step):
    rows = [partial[i * capacity : (i + 1) * capacity] for i in range(2 * experts)]
    near = [part.astype(jnp.bfloat16) for part in rows[experts:]]
    received = swap(jnp.concatenate(near[1:], axis=0), FAR).astype(jnp.float32)
    back = [
        to_section(rows[0].astype(jnp.bfloat16), step),
        to_section(near[0], step, lambda i: i ^ FAR),
    ]
    for r in range(1, experts):
        summed = rows[r] + received[(r - 1) * capacity : r * capacity]
        back.append(
            to_section(summed.astype(jnp.bfloat16), step, lambda i, r=r: i - SLICES * r)
        )
    return back


def collect(chooser, back, experts, capacity):
    chooser = chooser.astype(jnp.bfloat16)
    total = dot(chooser[:, :capacity], back[0]) + dot(chooser[:, :capacity], back[1])
    for r in range(1, experts):
        total = total + dot(chooser[:, r * capacity : (r + 1) * capacity], back[r + 1])
    return own_half_first(total)


def body(
    fwd_act,
    fwd_route,
    fwd_gate,
    bwd_act,
    bwd_grad,
    bwd_route,
    bwd_gate,
    norm_gain,
    w_gate,
    w_up,
    w_down,
):
    experts = lax.axis_size("ep") // SLICES
    tokens = fwd_act.shape[1]
    capacity = 2 * ((5 * tokens + 8 * experts - 1) // (8 * experts))
    half = w_gate.shape[2]
    gain = norm_gain[0][None, :]

    blocks = []
    for weight in (w_gate[0, 0], w_up[0, 0], w_down[0, 0]):
        beside = swap(weight, SIDE)
        blocks.append([[weight, swap(weight, NEAR)], [beside, swap(beside, NEAR)]])
    gates, ups, downs = blocks

    fwd_wide = fwd_act[0].astype(jnp.float32)
    fwd_normed = own_half_first((fwd_wide * inverse_rms(fwd_wide) * gain).astype(jnp.bfloat16))
    fwd_plan = slot_plan(fwd_route[0], experts, capacity)
    fwd_groups = [place(fwd_plan, r, capacity, fwd_normed) for r in range(experts)]
    fwd_x = jnp.concatenate(spread(fwd_groups), axis=0)

    bwd_wide = bwd_act[0].astype(jnp.float32)
    bwd_normed = own_half_first((bwd_wide * inverse_rms(bwd_wide) * gain).astype(jnp.bfloat16))
    weighted = own_half_first((bwd_gate[0] * bwd_grad[0].astype(jnp.float32)).astype(jnp.bfloat16))
    bwd_plan = slot_plan(bwd_route[0], experts, capacity)
    bwd_groups = [
        jnp.concatenate(
            [place(bwd_plan, r, capacity, bwd_normed), place(bwd_plan, r, capacity, weighted)], axis=0
        )
        for r in range(experts)
    ]
    bwd_arrived = spread(bwd_groups)
    bwd_x = jnp.concatenate([part[:capacity] for part in bwd_arrived], axis=0)
    bwd_g = jnp.concatenate([part[capacity:] for part in bwd_arrived], axis=0)

    fwd_base = to_section(fwd_act[0], 1)
    fwd_mix = to_section(fwd_plan.astype(jnp.float32) * fwd_gate[0], 1)
    bwd_base = to_section(bwd_act[0], -1)
    bwd_seed = to_section(bwd_grad[0], -1)
    bwd_mix = to_section(bwd_plan.astype(jnp.bfloat16), -1)

    def project(rows, pair):
        return dot(rows[:, :half], pair[0]) + dot(rows[:, half:], pair[1])

    hidden = []
    for j in range(2):
        pre = project(fwd_x, gates[j])
        hidden.append((jax.nn.silu(pre) * project(fwd_x, ups[j])).astype(jnp.bfloat16))
    fwd_out = jnp.concatenate(
        [dot(hidden[0], downs[0][k]) + dot(hidden[1], downs[1][k]) for k in range(2)], axis=1
    )
    fwd_back = send_back(fwd_out, experts, capacity, 1)

    d_gates, d_ups = [], []
    for j in range(2):
        pre = project(bwd_x, gates[j])
        up = project(bwd_x, ups[j])
        d_hidden = dot_t(bwd_g[:, :half], downs[j][0]) + dot_t(bwd_g[:, half:], downs[j][1])
        logistic = jax.nn.sigmoid(pre)
        d_gates.append(
            (d_hidden * up * logistic * (1.0 + pre * (1.0 - logistic))).astype(jnp.bfloat16)
        )
        d_ups.append((d_hidden * pre * logistic).astype(jnp.bfloat16))
    d_out = jnp.concatenate(
        [
            dot_t(d_gates[0], gates[0][k])
            + dot_t(d_ups[0], ups[0][k])
            + dot_t(d_gates[1], gates[1][k])
            + dot_t(d_ups[1], ups[1][k])
            for k in range(2)
        ],
        axis=1,
    )
    bwd_back = send_back(own_half_first(gain) * d_out, experts, capacity, -1)

    fwd_weight = jnp.sum(fwd_mix, axis=1, keepdims=True)
    fwd_mixed = collect(fwd_mix > 0, fwd_back, experts, capacity)
    fwd_next = (fwd_base.astype(jnp.float32) + fwd_weight * fwd_mixed).astype(jnp.bfloat16)

    scaled = collect(bwd_mix, bwd_back, experts, capacity)
    widened = bwd_base.astype(jnp.float32)
    inverse = inverse_rms(widened)
    bwd_next = (
        bwd_seed.astype(jnp.float32)
        + scaled * inverse
        - widened * (inverse * inverse * inverse) * jnp.mean(scaled * widened, axis=-1, keepdims=True)
    ).astype(jnp.bfloat16)
    return (fwd_next[None], bwd_next[None])


def solution(mesh):
    rows = P("pp", "ep", None)
    weights = P("pp", "ep", None, None)
    in_specs = (rows,) * 7 + (P("pp", None),) + (weights,) * 3
    return jax.shard_map(
        body, mesh=mesh, in_specs=in_specs, out_specs=(rows, rows), check_vma=False
    )
```

```python
import functools

import jax
import jax.numpy as jnp
from jax import lax
from jax.experimental import pallas as pl
from jax.experimental.pallas import tpu as pltpu
from jax.sharding import PartitionSpec as P

SLICES = 8
NEAR, SIDE, FAR = 1, 2, 4
SHORT, LONG = 10**9, 2 * 10**11


def swap(value, bit):
    return lax.ppermute(value, "ep", [(i, i ^ bit) for i in range(lax.axis_size("ep"))])


def to_expert(value, shift):
    count = lax.axis_size("ep")
    return lax.ppermute(value, "ep", [(i, (i + SLICES * shift) % count) for i in range(count)])


def to_section(value, step, place=lambda i: i):
    sections, count = lax.axis_size("pp"), lax.axis_size("ep")
    pairs = [
        (p * count + i, (p + step) % sections * count + place(i) % count)
        for p in range(sections)
        for i in range(count)
    ]
    return lax.ppermute(value, ("pp", "ep"), pairs)


def after(value, *done):
    return lax.optimization_barrier((value, done))[0]


def dot(a, b):
    return jnp.dot(a, b, preferred_element_type=jnp.float32)


def dot_t(a, b):
    return lax.dot_general(a, b, (((1,), (1,)), ((), ())), preferred_element_type=jnp.float32)


def dot_first(a, b):
    return lax.dot_general(a, b, (((0,), (0,)), ((), ())), preferred_element_type=jnp.float32)


def call(kernel, name, outs, cost, args):
    def whole(shape):
        return pl.BlockSpec(shape, lambda i: (0, 0))

    return pl.pallas_call(
        kernel,
        name=name,
        grid=(1,),
        out_shape=[jax.ShapeDtypeStruct(shape, jnp.bfloat16) for shape in outs],
        in_specs=[whole(arg.shape) for arg in args],
        out_specs=[whole(shape) for shape in outs],
        cost_estimate=pl.CostEstimate(flops=cost, bytes_accessed=0, transcendentals=0),
        compiler_params=pltpu.CompilerParams(vmem_limit_bytes=24 * 2**20),
    )(*args)


def my_place():
    me = lax.axis_index("ep")
    return me // SLICES, me % 2


def slot_rows(route_ref, mine, experts, capacity):
    chosen = route_ref[...]
    tokens = chosen.shape[1]
    onehot = lax.broadcasted_iota(jnp.int32, (experts, tokens), 0) == chosen
    before = lax.broadcasted_iota(jnp.int32, (tokens, tokens), 0) <= lax.broadcasted_iota(
        jnp.int32, (tokens, tokens), 1
    )
    running = dot(onehot.astype(jnp.bfloat16), before.astype(jnp.bfloat16))
    position = jnp.sum(jnp.where(onehot, running, 0.0), axis=0, keepdims=True) - 1.0
    relative = chosen - mine
    relative = jnp.where(relative < 0, relative + experts, relative)
    return relative * capacity + position.astype(jnp.int32)


def choose(target, first, count):
    slots = lax.broadcasted_iota(jnp.int32, (count, target.shape[1]), 0)
    return slots == target - first


def to_column(row):
    size = row.shape[1]
    same = lax.broadcasted_iota(jnp.int32, (size, size), 0) == lax.broadcasted_iota(
        jnp.int32, (size, size), 1
    )
    return jnp.sum(jnp.where(same, row, 0.0), axis=1, keepdims=True)


def inverse_rms(widened):
    return lax.rsqrt(jnp.mean(widened * widened, axis=-1, keepdims=True) + 1e-06)


def put_halves(out_ref, first, core, chooser, rows):
    half = rows.shape[1] // 2
    for k in range(2):
        placed = dot(chooser, rows[:, k * half : (k + 1) * half]).astype(jnp.bfloat16)
        start = first + half * (core if k == 0 else 1 - core)
        out_ref[:, pl.ds(pl.multiple_of(start, 128), half)] = placed


def token_slots(target, count, lanes):
    column = to_column(target.astype(jnp.float32)).astype(jnp.int32)
    return lax.broadcasted_iota(jnp.int32, (target.shape[1], lanes), 1) == column


def prepare_kernel(experts, capacity, route_ref, gate_ref, act_ref, gain_ref, pack_ref, *outs):
    mine, core = my_place()
    width = act_ref.shape[1]
    target = slot_rows(route_ref, mine, experts, capacity)
    widened = act_ref[...].astype(jnp.float32)
    normed = (widened * inverse_rms(widened) * gain_ref[...]).astype(jnp.bfloat16)
    for r in range(experts):
        chooser = choose(target, r * capacity, capacity).astype(jnp.bfloat16)
        put_halves(outs[r], 0, core, chooser, normed)
    pack_ref[:, :width] = act_ref[...]
    lanes = pack_ref.shape[1] - width
    slots = experts * capacity
    packed = token_slots(target, slots, lanes).astype(jnp.float32)
    rest = to_column(gate_ref[...])
    lane = lax.broadcasted_iota(jnp.int32, packed.shape, 1)
    for part in range(3):
        piece = rest.astype(jnp.bfloat16).astype(jnp.float32)
        packed = jnp.where(lane == slots + part, piece, packed)
        rest = rest - piece
    pack_ref[:, width:] = packed.astype(jnp.bfloat16)


def prepare_back_kernel(
    experts, capacity, route_ref, gate_ref, act_ref, grad_ref, gain_ref, pack_ref, *outs
):
    mine, core = my_place()
    width = act_ref.shape[1]
    target = slot_rows(route_ref, mine, experts, capacity)
    widened = act_ref[...].astype(jnp.float32)
    normed = (widened * inverse_rms(widened) * gain_ref[...]).astype(jnp.bfloat16)
    weighted = (to_column(gate_ref[...]) * grad_ref[...].astype(jnp.float32)).astype(jnp.bfloat16)
    for r in range(experts):
        chooser = choose(target, r * capacity, capacity).astype(jnp.bfloat16)
        if r == 0:
            put_halves(outs[0], 0, core, chooser, normed)
            put_halves(outs[1], 0, core, chooser, weighted)
        else:
            put_halves(outs[r + 1], 0, core, chooser, normed)
            put_halves(outs[r + 1], width, core, chooser, weighted)
    pack_ref[:, :width] = act_ref[...]
    pack_ref[:, width : 2 * width] = grad_ref[...]
    lanes = pack_ref.shape[1] - 2 * width
    packed = token_slots(target, experts * capacity, lanes)
    pack_ref[:, 2 * width :] = packed.astype(jnp.float32).astype(jnp.bfloat16)


def join_kernel(*refs):
    *parts, out_ref = refs
    width = parts[0].shape[1]
    for i, part in enumerate(parts):
        out_ref[:, i * width : (i + 1) * width] = part[...]


def collected(chooser, core, back, capacity, k):
    half = back[0].shape[1] // 2
    start = pl.multiple_of(half * (core if k == 0 else 1 - core), 128)
    columns = pl.ds(start, half)
    first = chooser[:, :capacity]
    total = dot(first, back[0][:, columns]) + dot(first, back[1][:, columns])
    for r, part in enumerate(back[2:], 1):
        total = total + dot(chooser[:, r * capacity : (r + 1) * capacity], part[:, columns])
    return total


def finish_kernel(experts, capacity, pack_ref, *rest):
    *back, out_ref = rest
    core = my_place()[1]
    width = out_ref.shape[1]
    half = width // 2
    slots = experts * capacity
    packed = pack_ref[:, width:]
    parts = packed[:, slots : slots + 3].astype(jnp.float32)
    weight = parts[:, 0:1] + parts[:, 1:2] + parts[:, 2:3]
    for k in range(2):
        columns = slice(k * half, (k + 1) * half)
        mixed = collected(packed, core, back, capacity, k)
        out_ref[:, columns] = (
            pack_ref[:, columns].astype(jnp.float32) + weight * mixed
        ).astype(jnp.bfloat16)


def finish_back_kernel(experts, capacity, pack_ref, *rest):
    *back, out_ref = rest
    core = my_place()[1]
    width = out_ref.shape[1]
    half = width // 2
    packed = pack_ref[:, 2 * width :]
    scaled = [collected(packed, core, back, capacity, k) for k in range(2)]
    widened = [pack_ref[:, k * half : (k + 1) * half].astype(jnp.float32) for k in range(2)]
    squares = sum(jnp.sum(w * w, axis=-1, keepdims=True) for w in widened)
    inverse = lax.rsqrt(squares / width + 1e-06)
    inner = sum(jnp.sum(s * w, axis=-1, keepdims=True) for s, w in zip(scaled, widened))
    factor = inverse * inverse * inverse * (inner / width)
    for k in range(2):
        seed = pack_ref[:, width + k * half : width + (k + 1) * half].astype(jnp.float32)
        out_ref[:, k * half : (k + 1) * half] = (
            seed + scaled[k] * inverse - widened[k] * factor
        ).astype(jnp.bfloat16)


def send_back(partial, experts, capacity):
    near = partial[experts * capacity :].astype(jnp.bfloat16)
    return swap(near[capacity:], FAR), near[:capacity], partial[:capacity].astype(jnp.bfloat16)


def send_sums(partial, received, experts, capacity, step):
    sums = []
    for r in range(1, experts):
        part = received[(r - 1) * capacity : r * capacity].astype(jnp.float32)
        summed = (partial[r * capacity : (r + 1) * capacity] + part).astype(jnp.bfloat16)
        sums.append(to_section(summed, step, lambda i, r=r: i - SLICES * r))
    return sums


def body(
    fwd_act,
    fwd_route,
    fwd_gate,
    bwd_act,
    bwd_grad,
    bwd_route,
    bwd_gate,
    norm_gain,
    w_gate,
    w_up,
    w_down,
):
    experts = lax.axis_size("ep") // SLICES
    tokens, width = fwd_act.shape[1:]
    capacity = 2 * ((5 * tokens + 8 * experts - 1) // (8 * experts))
    half = w_gate.shape[2]
    shifts = range(1, experts)
    me = lax.axis_index("ep")
    gate, up, down = w_gate[0, 0], w_up[0, 0], w_down[0, 0]
    row = (1, tokens)
    lanes = -(-(experts * capacity + 3) // 128) * 128
    slots = (capacity, width)
    two_slots = (capacity, 2 * width)

    side_down = swap(down, SIDE)
    near_gate = swap(gate, NEAR)
    fwd_pack, *fwd_groups = call(
        functools.partial(prepare_kernel, experts, capacity),
        "prepare",
        [(tokens, width + lanes)] + [slots] * experts,
        LONG,
        (fwd_route.reshape(row), fwd_gate.reshape(row), fwd_act[0], norm_gain),
    )
    fwd_far = [to_expert(fwd_groups[r], r) for r in shifts]
    own_pairs = [swap(fwd_groups[0], FAR)]
    fwd_pack = to_section(fwd_pack, 1)
    bwd_pack, bwd_first, grad_first, *bwd_groups = call(
        functools.partial(prepare_back_kernel, experts, capacity),
        "prepare_back",
        [(tokens, 2 * width + lanes), slots, slots] + [two_slots] * (experts - 1),
        SHORT,
        (bwd_route.reshape(row), bwd_gate.reshape(row), bwd_act[0], bwd_grad[0], norm_gain),
    )

    first = (side_down, near_gate, fwd_pack, own_pairs[0], *fwd_far)
    near_up = swap(after(up, *first), NEAR)
    bwd_pack = to_section(after(bwd_pack, *first), -1)
    (mixed,) = call(
        join_kernel,
        "join",
        [(capacity, experts * width)],
        LONG,
        (after(bwd_first, *first), *fwd_far),
    )
    mixed_pair = swap(mixed, FAR)
    own_pairs.append(mixed_pair[:, :width])
    fwd_far_pair = [mixed_pair[:, r * width : (r + 1) * width] for r in shifts]
    side_gate = swap(after(gate, *first), SIDE)
    bwd_far = [to_expert(after(bwd_groups[r - 1], *first), r) for r in shifts]

    second = (side_gate, near_up, bwd_pack, mixed_pair, *bwd_far)
    side_near_down = swap(after(side_down, *second), NEAR)
    near_down = swap(after(down, *second), NEAR)
    side_near_gate = swap(after(side_gate, side_near_down), NEAR)
    own_pairs.append(swap(after(grad_first, *second), FAR))
    bwd_far_pair = [swap(after(part, *second), FAR) for part in bwd_far]
    side_up = swap(after(up, *second), SIDE)
    third = (side_up, near_down, side_near_gate, own_pairs[2], *bwd_far_pair)
    side_near_up = swap(after(side_up, *third), NEAR)

    gates = [[gate, near_gate], [side_gate, side_near_gate]]
    ups = [[up, near_up], [side_up, side_near_up]]
    downs = [[down, near_down], [side_down, side_near_down]]

    def joined(own, mine, own_pair, theirs, at):
        def part(value):
            return value[:, at * width : (at + 1) * width]

        return jnp.concatenate([own, *map(part, mine), own_pair, *map(part, theirs)], axis=0)

    fwd_x = joined(fwd_groups[0], fwd_far, own_pairs[0], fwd_far_pair, 0)
    bwd_x = joined(bwd_first, bwd_far, own_pairs[1], bwd_far_pair, 0)
    bwd_g = joined(grad_first, bwd_far, own_pairs[2], bwd_far_pair, 1)

    def project(rows, pair):
        return dot(rows[:, :half], pair[0]) + dot(rows[:, half:], pair[1])

    hidden = []
    for j in range(2):
        pre = project(fwd_x, gates[j])
        hidden.append((jax.nn.silu(pre) * project(fwd_x, ups[j])).astype(jnp.bfloat16))
    fwd_out = jnp.concatenate(
        [dot(hidden[0], downs[0][k]) + dot(hidden[1], downs[1][k]) for k in range(2)], axis=1
    )
    fwd_received, fwd_near, fwd_own = send_back(fwd_out, experts, capacity)
    fwd_near_sums = to_section(fwd_own, 1)

    d_gates, d_ups = [], []
    for j in range(2):
        pre = project(bwd_x, gates[j])
        upper = project(bwd_x, ups[j])
        d_hidden = dot_t(bwd_g[:, :half], downs[j][0]) + dot_t(bwd_g[:, half:], downs[j][1])
        logistic = jax.nn.sigmoid(pre)
        d_gates.append(
            (d_hidden * upper * logistic * (1.0 + pre * (1.0 - logistic))).astype(jnp.bfloat16)
        )
        d_ups.append((d_hidden * pre * logistic).astype(jnp.bfloat16))
    d_out = jnp.concatenate(
        [
            dot_t(d_gates[0], gates[0][k])
            + dot_t(d_ups[0], ups[0][k])
            + dot_t(d_gates[1], gates[1][k])
            + dot_t(d_ups[1], ups[1][k])
            for k in range(2)
        ],
        axis=1,
    )
    turned = jnp.concatenate([norm_gain[:, half:], norm_gain[:, :half]], axis=1)
    gain = jnp.where(me % 2 == 0, norm_gain, turned)
    d_out = gain * d_out
    bwd_received, bwd_near, bwd_own = send_back(d_out, experts, capacity)
    bwd_near_sums = to_section(bwd_own, -1)
    fwd_sums = send_sums(fwd_out, fwd_received, experts, capacity, 1)
    bwd_sums = send_sums(d_out, bwd_received, experts, capacity, -1)
    both = (fwd_received, bwd_received)
    fwd_second = to_section(after(fwd_near, *both), 1, lambda i: i ^ FAR)
    bwd_second = to_section(after(bwd_near, *both), -1, lambda i: i ^ FAR)
    fwd_back = (fwd_near_sums, fwd_second, *fwd_sums)
    bwd_back = (bwd_near_sums, bwd_second, *bwd_sums)

    (fwd_next,) = call(
        functools.partial(finish_kernel, experts, capacity),
        "finish",
        [(tokens, width)],
        SHORT,
        (fwd_pack, *fwd_back),
    )
    (bwd_next,) = call(
        functools.partial(finish_back_kernel, experts, capacity),
        "finish_back",
        [(tokens, width)],
        SHORT,
        (bwd_pack, *bwd_back),
    )
    return (fwd_next[None], bwd_next[None])


def solution(mesh):
    rows = P("pp", "ep", None)
    weights = P("pp", "ep", None, None)
    in_specs = (rows,) * 7 + (P("pp", None),) + (weights,) * 3
    return jax.shard_map(
        body, mesh=mesh, in_specs=in_specs, out_specs=(rows, rows), check_vma=False
    )
```

```python
import functools

import jax
import jax.numpy as jnp
from jax import lax
from jax.experimental import pallas as pl
from jax.experimental.pallas import tpu as pltpu
from jax.sharding import PartitionSpec as P

SLICES = 8
NEAR, SIDE, FAR = 1, 2, 4
SHORT, LONG = 10**6, 2 * 10**11
FULL = 58 * 2**20


def swap(value, bit):
    return lax.ppermute(value, "ep", [(i, i ^ bit) for i in range(lax.axis_size("ep"))])


def to_expert(value, shift):
    count = lax.axis_size("ep")
    return lax.ppermute(value, "ep", [(i, (i + SLICES * shift) % count) for i in range(count)])


def to_section(value, step, place=lambda i: i):
    sections, count = lax.axis_size("pp"), lax.axis_size("ep")
    pairs = [
        (p * count + i, (p + step) % sections * count + place(i) % count)
        for p in range(sections)
        for i in range(count)
    ]
    return lax.ppermute(value, ("pp", "ep"), pairs)


def after(value, *done):
    return lax.optimization_barrier((value, done))[0]


def dot(a, b):
    return jnp.dot(a, b, preferred_element_type=jnp.float32)


def dot_t(a, b):
    return lax.dot_general(a, b, (((1,), (1,)), ((), ())), preferred_element_type=jnp.float32)


def dot_first(a, b):
    return lax.dot_general(a, b, (((0,), (0,)), ((), ())), preferred_element_type=jnp.float32)


def call(kernel, name, outs, cost, args, held=4, scratch=()):
    space = pl.BlockSpec(memory_space=pltpu.VMEM)
    return pl.pallas_call(
        kernel,
        name=name,
        out_shape=[jax.ShapeDtypeStruct(shape, kind) for shape, kind in outs],
        in_specs=[space] * len(args),
        out_specs=[space] * len(outs),
        scratch_shapes=list(scratch),
        cost_estimate=pl.CostEstimate(flops=cost, bytes_accessed=0, transcendentals=0),
        compiler_params=pltpu.CompilerParams(vmem_limit_bytes=held * 2**20),
    )(*args)


def call_fetching(kernel, name, outs, cost, args):
    count = len(args)

    def fetching(*refs):
        sources, rest = refs[:count], refs[count : count + len(outs)]
        held, sems = refs[count + len(outs) : -1], refs[-1]
        copies = [
            pltpu.make_async_copy(source, target, sems.at[i])
            for i, (source, target) in enumerate(zip(sources, held))
        ]
        for copy in copies:
            copy.start()
        for copy in copies:
            copy.wait()
        kernel(*held, *rest)

    return pl.pallas_call(
        fetching,
        name=name,
        out_shape=[jax.ShapeDtypeStruct(shape, kind) for shape, kind in outs],
        in_specs=[pl.BlockSpec(memory_space=pltpu.HBM)] * count,
        out_specs=[pl.BlockSpec(memory_space=pltpu.VMEM)] * len(outs),
        scratch_shapes=[pltpu.VMEM(arg.shape, arg.dtype) for arg in args]
        + [pltpu.SemaphoreType.DMA((count,))],
        cost_estimate=pl.CostEstimate(flops=cost, bytes_accessed=0, transcendentals=0),
        compiler_params=pltpu.CompilerParams(vmem_limit_bytes=FULL),
    )(*args)


def my_place():
    me = lax.axis_index("ep")
    return me // SLICES, me % 2


def split_kernel(gate_ref, up_ref, large_ref, small_ref, sems):
    half, cut = gate_ref.shape[0], up_ref.shape[0] - small_ref.shape[0]
    copies = [
        pltpu.make_async_copy(gate_ref, large_ref.at[pl.ds(0, half)], sems.at[0]),
        pltpu.make_async_copy(up_ref.at[pl.ds(0, cut)], large_ref.at[pl.ds(half, cut)], sems.at[1]),
        pltpu.make_async_copy(up_ref.at[pl.ds(cut, half - cut)], small_ref, sems.at[2]),
    ]
    for copy in copies:
        copy.start()
    for copy in copies:
        copy.wait()


def split_weights(gate, up):
    half, units = up.shape
    cut = -(-half // 512) * 128
    anywhere = pl.BlockSpec(memory_space=pl.ANY)
    return pl.pallas_call(
        split_kernel,
        name="split_weights",
        out_shape=[
            jax.ShapeDtypeStruct((half + cut, units), up.dtype),
            jax.ShapeDtypeStruct((half - cut, units), up.dtype),
        ],
        in_specs=[anywhere] * 2,
        out_specs=[anywhere] * 2,
        scratch_shapes=[pltpu.SemaphoreType.DMA((3,))],
        cost_estimate=pl.CostEstimate(flops=SHORT, bytes_accessed=0, transcendentals=0),
        compiler_params=pltpu.CompilerParams(vmem_limit_bytes=2 * 2**20),
    )(gate, up)


def slot_rows(route_ref, mine, experts, capacity):
    chosen = route_ref[...]
    tokens = chosen.shape[1]
    onehot = lax.broadcasted_iota(jnp.int32, (experts, tokens), 0) == chosen
    before = lax.broadcasted_iota(jnp.int32, (tokens, tokens), 0) <= lax.broadcasted_iota(
        jnp.int32, (tokens, tokens), 1
    )
    running = dot(onehot.astype(jnp.bfloat16), before.astype(jnp.bfloat16))
    position = jnp.sum(jnp.where(onehot, running, 0.0), axis=0, keepdims=True) - 1.0
    relative = chosen - mine
    relative = jnp.where(relative < 0, relative + experts, relative)
    return relative * capacity + position.astype(jnp.int32)


def choose(target, first, count):
    slots = lax.broadcasted_iota(jnp.int32, (count, target.shape[1]), 0)
    return slots == target - first


def to_column(row):
    size = row.shape[1]
    same = lax.broadcasted_iota(jnp.int32, (size, size), 0) == lax.broadcasted_iota(
        jnp.int32, (size, size), 1
    )
    return jnp.sum(jnp.where(same, row, 0.0), axis=1, keepdims=True)


def inverse_rms(widened):
    return lax.rsqrt(jnp.mean(widened * widened, axis=-1, keepdims=True) + 1e-06)


def put_halves(out_ref, first, core, chooser, rows):
    half = rows.shape[1] // 2
    for k in range(2):
        placed = dot(chooser, rows[:, k * half : (k + 1) * half]).astype(jnp.bfloat16)
        start = first + half * (core if k == 0 else 1 - core)
        out_ref[:, pl.ds(pl.multiple_of(start, 128), half)] = placed


def token_slots(target, count, lanes):
    column = to_column(target.astype(jnp.float32)).astype(jnp.int32)
    return lax.broadcasted_iota(jnp.int32, (target.shape[1], lanes), 1) == column


def prepare_kernel(experts, capacity, route_ref, gate_ref, act_ref, gain_ref, pack_ref, *outs):
    mine, core = my_place()
    width = act_ref.shape[1]
    target = slot_rows(route_ref, mine, experts, capacity)
    widened = act_ref[...].astype(jnp.float32)
    normed = (widened * inverse_rms(widened) * gain_ref[...]).astype(jnp.bfloat16)
    for r in range(experts):
        chooser = choose(target, r * capacity, capacity).astype(jnp.bfloat16)
        put_halves(outs[r], 0, core, chooser, normed)
    pack_ref[:, :width] = act_ref[...]
    lanes = pack_ref.shape[1] - width
    slots = experts * capacity
    packed = token_slots(target, slots, lanes).astype(jnp.float32)
    rest = to_column(gate_ref[...])
    lane = lax.broadcasted_iota(jnp.int32, packed.shape, 1)
    for part in range(3):
        piece = rest.astype(jnp.bfloat16).astype(jnp.float32)
        packed = jnp.where(lane == slots + part, piece, packed)
        rest = rest - piece
    pack_ref[:, width:] = packed.astype(jnp.bfloat16)


def prepare_back_kernel(
    experts, capacity, route_ref, gate_ref, act_ref, grad_ref, gain_ref, pack_ref, *outs
):
    mine, core = my_place()
    width = act_ref.shape[1]
    target = slot_rows(route_ref, mine, experts, capacity)
    widened = act_ref[...].astype(jnp.float32)
    normed = (widened * inverse_rms(widened) * gain_ref[...]).astype(jnp.bfloat16)
    weighted = (to_column(gate_ref[...]) * grad_ref[...].astype(jnp.float32)).astype(jnp.bfloat16)
    for r in range(experts):
        chooser = choose(target, r * capacity, capacity).astype(jnp.bfloat16)
        if r == 0:
            put_halves(outs[0], 0, core, chooser, normed)
            put_halves(outs[1], 0, core, chooser, weighted)
        else:
            put_halves(outs[r + 1], 0, core, chooser, normed)
            put_halves(outs[r + 1], width, core, chooser, weighted)
    pack_ref[:, :width] = act_ref[...]
    pack_ref[:, width : 2 * width] = grad_ref[...]
    lanes = pack_ref.shape[1] - 2 * width
    packed = token_slots(target, experts * capacity, lanes)
    pack_ref[:, 2 * width :] = packed.astype(jnp.float32).astype(jnp.bfloat16)


def join_kernel(*refs):
    *parts, out_ref = refs
    start = 0
    for part in parts:
        out_ref[:, start : start + part.shape[1]] = part[...]
        start += part.shape[1]


def collected(chooser, core, back, capacity, k):
    half = back[0].shape[1] // 2
    start = pl.multiple_of(half * (core if k == 0 else 1 - core), 128)
    columns = pl.ds(start, half)
    first = chooser[:, :capacity]
    total = dot(first, back[0][:, columns]) + dot(first, back[1][:, columns])
    for r, part in enumerate(back[2:], 1):
        total = total + dot(chooser[:, r * capacity : (r + 1) * capacity], part[:, columns])
    return total


def finish_kernel(experts, capacity, pack_ref, *rest):
    *back, out_ref = rest
    core = my_place()[1]
    width = out_ref.shape[1]
    half = width // 2
    slots = experts * capacity
    packed = pack_ref[:, width:]
    parts = packed[:, slots : slots + 3].astype(jnp.float32)
    weight = parts[:, 0:1] + parts[:, 1:2] + parts[:, 2:3]
    for k in range(2):
        columns = slice(k * half, (k + 1) * half)
        mixed = collected(packed, core, back, capacity, k)
        out_ref[:, columns] = (
            pack_ref[:, columns].astype(jnp.float32) + weight * mixed
        ).astype(jnp.bfloat16)


def finish_back_kernel(experts, capacity, pack_ref, *rest):
    *back, out_ref = rest
    core = my_place()[1]
    width = out_ref.shape[1]
    half = width // 2
    packed = pack_ref[:, 2 * width :]
    scaled = [collected(packed, core, back, capacity, k) for k in range(2)]
    widened = [pack_ref[:, k * half : (k + 1) * half].astype(jnp.float32) for k in range(2)]
    squares = sum(jnp.sum(w * w, axis=-1, keepdims=True) for w in widened)
    inverse = lax.rsqrt(squares / width + 1e-06)
    inner = sum(jnp.sum(s * w, axis=-1, keepdims=True) for s, w in zip(scaled, widened))
    factor = inverse * inverse * inverse * (inner / width)
    for k in range(2):
        seed = pack_ref[:, width + k * half : width + (k + 1) * half].astype(jnp.float32)
        out_ref[:, k * half : (k + 1) * half] = (
            seed + scaled[k] * inverse - widened[k] * factor
        ).astype(jnp.bfloat16)


def up_rows(block, half, begin, end):
    large, small, _ = block
    cut = large.shape[0] - half
    return large[half + begin : half + end] if begin < cut else small[begin - cut : end - cut]


def row_ranges(blocks, half):
    cut = max(block[0].shape[0] - half for block in blocks)
    return ((0, cut), (cut, half)) if cut else ((0, half),)


def activations(x_ref, blocks):
    half = x_ref.shape[1] // 2
    pre, upper = 0.0, 0.0
    for k, block in enumerate(blocks):
        first = k * half
        pre = pre + dot(x_ref[:, first : first + half], block[0][:half])
        for begin, end in row_ranges(blocks, half):
            columns = slice(first + begin, first + end)
            upper = upper + dot(x_ref[:, columns], up_rows(block, half, begin, end))
    return pre, upper


def stack_rows(out_ref, pieces):
    width = out_ref.shape[1]
    step = width // 4
    for first in range(0, width, step):
        parts = [ref[:, at + first : at + first + step].astype(jnp.float32) for ref, at in pieces]
        out_ref[:, first : first + step] = jnp.concatenate(parts, axis=0).astype(jnp.bfloat16)


def forward_near_kernel(experts, *refs):
    *near, pair_ref = refs[: experts + 2]
    blocks = refs[experts + 2 : experts + 5], refs[experts + 5 : experts + 8]
    x_ref, part_ref = refs[experts + 8 :]
    pieces = [(ref, 0) for ref in near]
    stack_rows(x_ref, pieces + [(pair_ref, r * x_ref.shape[1]) for r in range(experts - 1)])
    pre, upper = activations(x_ref, blocks)
    hidden = (jax.nn.silu(pre) * upper).astype(jnp.bfloat16)
    half = x_ref.shape[1] // 2
    for k in range(2):
        part_ref[:, k * half : (k + 1) * half] = dot(hidden, blocks[k][2][...])


def put_rows(capacity, total, first, own_ref, near_ref, cross_ref, far_ref):
    columns = slice(first, first + total.shape[1])
    count = total.shape[0] // 2
    own_ref[:, columns] = total[:capacity].astype(jnp.bfloat16)
    far_ref[:, columns] = total[capacity:count]
    near_ref[:, columns] = total[count : count + capacity].astype(jnp.bfloat16)
    cross_ref[:, columns] = total[count + capacity :].astype(jnp.bfloat16)


def forward_side_kernel(capacity, x_ref, part_ref, *refs):
    blocks, outs = (refs[:3], refs[3:6]), refs[6:]
    pre, upper = activations(x_ref, blocks)
    hidden = (jax.nn.silu(pre) * upper).astype(jnp.bfloat16)
    half = x_ref.shape[1] // 2
    for k in range(2):
        total = part_ref[:, k * half : (k + 1) * half] + dot(hidden, blocks[k][2][...])
        put_rows(capacity, total, k * half, *outs)


def backward_kernel(experts, capacity, *refs):
    core = my_place()[1]
    first_ref, grad_ref, *far_refs = refs[: experts + 1]
    pair_ref, rest_ref, gain_ref = refs[experts + 1 : experts + 4]
    blocks = refs[experts + 4 : experts + 16]
    *outs, x_ref, g_ref = refs[experts + 16 :]
    sets = [(blocks[i : i + 3], blocks[i + 3 : i + 6]) for i in (0, 6)]
    width = first_ref.shape[1]
    half = width // 2
    ahead = [(ref, 0) for ref in (first_ref, *far_refs)] + [(pair_ref, pair_ref.shape[1] - width)]
    stack_rows(x_ref, ahead + [(rest_ref, (2 * r - 1) * width) for r in range(1, experts)])
    behind = [(grad_ref, 0)] + [(ref, width) for ref in far_refs] + [(rest_ref, 0)]
    stack_rows(g_ref, behind + [(rest_ref, 2 * r * width) for r in range(1, experts)])
    steps = []
    for blocks in sets:
        pre, upper = activations(x_ref, blocks)
        d_hidden = sum(
            dot_t(g_ref[:, k * half : (k + 1) * half], blocks[k][2][...]) for k in range(2)
        )
        logistic = jax.nn.sigmoid(pre)
        d_gate = d_hidden * upper * logistic * (1.0 + pre * (1.0 - logistic))
        d_up = d_hidden * pre * logistic
        steps.append((d_gate.astype(jnp.bfloat16), d_up.astype(jnp.bfloat16)))
    for k in range(2):
        for begin, end in row_ranges(sets[1], half):
            total = 0.0
            for (d_gate, d_up), blocks in zip(steps, sets):
                upper = up_rows(blocks[k], half, begin, end)
                total = total + dot_t(d_gate, blocks[k][0][begin:end]) + dot_t(d_up, upper)
            start = half * (core if k == 0 else 1 - core) + begin
            gain = gain_ref[:, pl.ds(pl.multiple_of(start, 128), end - begin)]
            put_rows(capacity, gain * total, k * half + begin, *outs)


def send_sums(far, received, experts, capacity, step):
    sums = []
    for r in range(1, experts):
        rows = slice((r - 1) * capacity, r * capacity)
        summed = (far[rows] + received[rows].astype(jnp.float32)).astype(jnp.bfloat16)
        sums.append(to_section(summed, step, lambda i, r=r: i - SLICES * r))
    return sums


def body(
    fwd_act,
    fwd_route,
    fwd_gate,
    bwd_act,
    bwd_grad,
    bwd_route,
    bwd_gate,
    norm_gain,
    w_gate,
    w_up,
    w_down,
):
    experts = lax.axis_size("ep") // SLICES
    tokens, width = fwd_act.shape[1:]
    capacity = 2 * ((5 * tokens + 8 * experts - 1) // (8 * experts))
    shifts = range(1, experts)
    gate, up, down = w_gate[0, 0], w_up[0, 0], w_down[0, 0]
    row = (1, tokens)
    lanes = -(-(experts * capacity + 3) // 128) * 128
    slots = ((capacity, width), jnp.bfloat16)
    two_slots = ((capacity, 2 * width), jnp.bfloat16)

    large, small = split_weights(gate, up)
    side_down = swap(down, SIDE)
    near_down = swap(down, NEAR)
    near_gate = swap(gate, NEAR)
    fwd_pack, *fwd_groups = call_fetching(
        functools.partial(prepare_kernel, experts, capacity),
        "prepare",
        [((tokens, width + lanes), jnp.bfloat16)] + [slots] * experts,
        LONG,
        (fwd_route.reshape(row), fwd_gate.reshape(row), fwd_act[0], norm_gain),
    )
    fwd_far = [to_expert(fwd_groups[r], r) for r in shifts]
    first_pair = swap(fwd_groups[0], FAR)
    bwd_pack, bwd_first, grad_first, *bwd_groups = call(
        functools.partial(prepare_back_kernel, experts, capacity),
        "prepare_back",
        [((tokens, 2 * width + lanes), jnp.bfloat16), slots, slots] + [two_slots] * (experts - 1),
        SHORT,
        (bwd_route.reshape(row), bwd_gate.reshape(row), bwd_act[0], bwd_grad[0], norm_gain),
        held=8,
    )

    first = (side_down, near_down, near_gate, first_pair, bwd_first, large, *fwd_far)
    fwd_pack = to_section(after(fwd_pack, *first), 1)
    near_up = swap(after(up, *first), NEAR)
    (mixed,) = call(
        join_kernel,
        "join",
        [((capacity, experts * width), jnp.bfloat16)],
        SHORT,
        (*after(tuple(fwd_far), *first), bwd_first),
    )
    own_pair = swap(mixed, FAR)
    side_large = swap(after(large, *first), SIDE)
    bwd_far = [to_expert(after(bwd_groups[r - 1], *first), r) for r in shifts]

    (rest,) = call(
        join_kernel,
        "join_back",
        [((capacity, (2 * experts - 1) * width), jnp.bfloat16)],
        LONG,
        (after(grad_first, side_large), *bwd_far),
    )
    second = (rest, fwd_pack, near_up, own_pair)
    rest_pair = swap(rest, FAR)
    bwd_pack = to_section(after(bwd_pack, *second), -1)
    side_small = swap(after(small, *second), SIDE)
    side_near_large = swap(after(side_large, *second), NEAR)
    side_near_down = swap(after(side_down, *second), NEAR)
    mine = ((gate, up, down), (near_gate, near_up, near_down))

    rows = (2 * experts * capacity, width)
    far = ((experts - 1) * capacity, width)
    outs = [slots, slots, (far, jnp.bfloat16), (far, jnp.float32)]
    pieces = after((fwd_groups[0], *fwd_far, first_pair, own_pair), rest, side_near_down)
    fwd_x, part = call(
        functools.partial(forward_near_kernel, experts),
        "forward_near",
        [(rows, jnp.bfloat16), (rows, jnp.float32)],
        SHORT,
        (*pieces, *mine[0], *mine[1]),
        held=6,
    )
    side_near_small = swap(after(side_small, part, side_near_large), NEAR)
    beside = ((side_large, side_small, side_down), (side_near_large, side_near_small, side_near_down))
    fwd_own, fwd_near, fwd_cross, fwd_sum = call(
        functools.partial(forward_side_kernel, capacity),
        "forward_side",
        outs,
        SHORT,
        (fwd_x, part, *beside[0], *beside[1]),
        held=6,
    )
    fwd_own, fwd_near, fwd_cross, fwd_sum, rest_pair, bwd_pack = lax.optimization_barrier(
        (fwd_own, fwd_near, fwd_cross, fwd_sum, rest_pair, bwd_pack)
    )
    fwd_received = swap(fwd_cross, FAR)
    fwd_near_sums = to_section(fwd_own, 1)
    fwd_second = to_section(fwd_near, 1, lambda i: i ^ FAR)

    bwd_own, bwd_near, bwd_cross, bwd_sum = call(
        functools.partial(backward_kernel, experts, capacity),
        "backward",
        outs,
        SHORT,
        (bwd_first, grad_first, *bwd_far, own_pair, rest_pair, norm_gain)
        + (*mine[0], *mine[1], *beside[0], *beside[1]),
        held=10,
        scratch=(pltpu.VMEM(rows, jnp.bfloat16),) * 2,
    )
    bwd_received = swap(bwd_cross, FAR)
    fwd_sums = send_sums(fwd_sum, fwd_received, experts, capacity, 1)
    bwd_near_sums = to_section(after(bwd_own, fwd_received), -1)
    bwd_sums = send_sums(bwd_sum, bwd_received, experts, capacity, -1)
    both = (fwd_received, bwd_received)
    bwd_second = to_section(after(bwd_near, *both), -1, lambda i: i ^ FAR)
    fwd_back = (fwd_near_sums, fwd_second, *fwd_sums)
    bwd_back = (bwd_near_sums, bwd_second, *bwd_sums)

    (fwd_next,) = call(
        functools.partial(finish_kernel, experts, capacity),
        "finish",
        [((tokens, width), jnp.bfloat16)],
        SHORT,
        (fwd_pack, *fwd_back),
        held=8,
    )
    (bwd_next,) = call(
        functools.partial(finish_back_kernel, experts, capacity),
        "finish_back",
        [((tokens, width), jnp.bfloat16)],
        SHORT,
        (bwd_pack, *bwd_back),
        held=8,
    )
    return (fwd_next[None], bwd_next[None])


def solution(mesh):
    rows = P("pp", "ep", None)
    weights = P("pp", "ep", None, None)
    in_specs = (rows,) * 7 + (P("pp", None),) + (weights,) * 3
    return jax.shard_map(
        body, mesh=mesh, in_specs=in_specs, out_specs=(rows, rows), check_vma=False
    )
```

```python
import functools

import jax
import jax.numpy as jnp
from jax import lax
from jax.experimental import pallas as pl
from jax.experimental.pallas import tpu as pltpu
from jax.sharding import PartitionSpec as P

SLICES = 8
NEAR, SIDE, FAR = 1, 2, 4
SHORT, LONG = 10**6, 2 * 10**11
FULL = 58 * 2**20


def swap(value, bit):
    return lax.ppermute(value, "ep", [(i, i ^ bit) for i in range(lax.axis_size("ep"))])


def to_expert(value, shift):
    count = lax.axis_size("ep")
    return lax.ppermute(value, "ep", [(i, (i + SLICES * shift) % count) for i in range(count)])


def to_section(value, step, place=lambda i: i):
    sections, count = lax.axis_size("pp"), lax.axis_size("ep")
    pairs = [
        (p * count + i, (p + step) % sections * count + place(i) % count)
        for p in range(sections)
        for i in range(count)
    ]
    return lax.ppermute(value, ("pp", "ep"), pairs)


def after(value, *done):
    return lax.optimization_barrier((value, done))[0]


def dot(a, b):
    return jnp.dot(a, b, preferred_element_type=jnp.float32)


def dot_t(a, b):
    return lax.dot_general(a, b, (((1,), (1,)), ((), ())), preferred_element_type=jnp.float32)


def dot_first(a, b):
    return lax.dot_general(a, b, (((0,), (0,)), ((), ())), preferred_element_type=jnp.float32)


def call(kernel, name, outs, cost, args, held=4, scratch=()):
    space = pl.BlockSpec(memory_space=pltpu.VMEM)
    return pl.pallas_call(
        kernel,
        name=name,
        out_shape=[jax.ShapeDtypeStruct(shape, kind) for shape, kind in outs],
        in_specs=[space] * len(args),
        out_specs=[space] * len(outs),
        scratch_shapes=list(scratch),
        cost_estimate=pl.CostEstimate(flops=cost, bytes_accessed=0, transcendentals=0),
        compiler_params=pltpu.CompilerParams(vmem_limit_bytes=held * 2**20),
    )(*args)


def call_fetching(kernel, name, outs, cost, args):
    count = len(args)

    def fetching(*refs):
        sources, rest = refs[:count], refs[count : count + len(outs)]
        held, sems = refs[count + len(outs) : -1], refs[-1]
        copies = [
            pltpu.make_async_copy(source, target, sems.at[i])
            for i, (source, target) in enumerate(zip(sources, held))
        ]
        for copy in copies:
            copy.start()
        for copy in copies:
            copy.wait()
        kernel(*held, *rest)

    return pl.pallas_call(
        fetching,
        name=name,
        out_shape=[jax.ShapeDtypeStruct(shape, kind) for shape, kind in outs],
        in_specs=[pl.BlockSpec(memory_space=pltpu.HBM)] * count,
        out_specs=[pl.BlockSpec(memory_space=pltpu.VMEM)] * len(outs),
        scratch_shapes=[pltpu.VMEM(arg.shape, arg.dtype) for arg in args]
        + [pltpu.SemaphoreType.DMA((count,))],
        cost_estimate=pl.CostEstimate(flops=cost, bytes_accessed=0, transcendentals=0),
        compiler_params=pltpu.CompilerParams(vmem_limit_bytes=FULL),
    )(*args)


def my_place():
    me = lax.axis_index("ep")
    return me // SLICES, me % 2


def split_kernel(gate_ref, up_ref, large_ref, small_ref, sems):
    half, cut = gate_ref.shape[0], up_ref.shape[0] - small_ref.shape[0]
    copies = [
        pltpu.make_async_copy(gate_ref, large_ref.at[pl.ds(0, half)], sems.at[0]),
        pltpu.make_async_copy(up_ref.at[pl.ds(0, cut)], large_ref.at[pl.ds(half, cut)], sems.at[1]),
        pltpu.make_async_copy(up_ref.at[pl.ds(cut, half - cut)], small_ref, sems.at[2]),
    ]
    for copy in copies:
        copy.start()
    for copy in copies:
        copy.wait()


def split_weights(gate, up):
    half, units = up.shape
    cut = half * 3 // 7 // 128 * 128
    anywhere = pl.BlockSpec(memory_space=pl.ANY)
    return pl.pallas_call(
        split_kernel,
        name="split_weights",
        out_shape=[
            jax.ShapeDtypeStruct((half + cut, units), up.dtype),
            jax.ShapeDtypeStruct((half - cut, units), up.dtype),
        ],
        in_specs=[anywhere] * 2,
        out_specs=[anywhere] * 2,
        scratch_shapes=[pltpu.SemaphoreType.DMA((3,))],
        cost_estimate=pl.CostEstimate(flops=SHORT, bytes_accessed=0, transcendentals=0),
        compiler_params=pltpu.CompilerParams(vmem_limit_bytes=2 * 2**20),
    )(gate, up)


def slot_rows(route_ref, mine, experts, capacity):
    chosen = route_ref[...]
    tokens = chosen.shape[1]
    onehot = lax.broadcasted_iota(jnp.int32, (experts, tokens), 0) == chosen
    before = lax.broadcasted_iota(jnp.int32, (tokens, tokens), 0) <= lax.broadcasted_iota(
        jnp.int32, (tokens, tokens), 1
    )
    running = dot(onehot.astype(jnp.bfloat16), before.astype(jnp.bfloat16))
    position = jnp.sum(jnp.where(onehot, running, 0.0), axis=0, keepdims=True) - 1.0
    relative = chosen - mine
    relative = jnp.where(relative < 0, relative + experts, relative)
    return relative * capacity + position.astype(jnp.int32)


def choose(target, first, count):
    slots = lax.broadcasted_iota(jnp.int32, (count, target.shape[1]), 0)
    return slots == target - first


def to_column(row):
    size = row.shape[1]
    same = lax.broadcasted_iota(jnp.int32, (size, size), 0) == lax.broadcasted_iota(
        jnp.int32, (size, size), 1
    )
    return jnp.sum(jnp.where(same, row, 0.0), axis=1, keepdims=True)


def inverse_rms(widened):
    return lax.rsqrt(jnp.mean(widened * widened, axis=-1, keepdims=True) + 1e-06)


def put_halves(out_ref, first, core, chooser, rows):
    half = rows.shape[1] // 2
    for k in range(2):
        placed = dot(chooser, rows[:, k * half : (k + 1) * half]).astype(jnp.bfloat16)
        start = first + half * (core if k == 0 else 1 - core)
        out_ref[:, pl.ds(pl.multiple_of(start, 128), half)] = placed


def token_slots(target, count, lanes):
    column = to_column(target.astype(jnp.float32)).astype(jnp.int32)
    return lax.broadcasted_iota(jnp.int32, (target.shape[1], lanes), 1) == column


def prepare_kernel(experts, capacity, route_ref, gate_ref, act_ref, gain_ref, pack_ref, *outs):
    mine, core = my_place()
    width = act_ref.shape[1]
    target = slot_rows(route_ref, mine, experts, capacity)
    widened = act_ref[...].astype(jnp.float32)
    normed = (widened * inverse_rms(widened) * gain_ref[...]).astype(jnp.bfloat16)
    for r in range(experts):
        chooser = choose(target, r * capacity, capacity).astype(jnp.bfloat16)
        put_halves(outs[r], 0, core, chooser, normed)
    pack_ref[:, :width] = act_ref[...]
    lanes = pack_ref.shape[1] - width
    slots = experts * capacity
    packed = token_slots(target, slots, lanes).astype(jnp.float32)
    rest = to_column(gate_ref[...])
    lane = lax.broadcasted_iota(jnp.int32, packed.shape, 1)
    for part in range(3):
        piece = rest.astype(jnp.bfloat16).astype(jnp.float32)
        packed = jnp.where(lane == slots + part, piece, packed)
        rest = rest - piece
    pack_ref[:, width:] = packed.astype(jnp.bfloat16)


def prepare_back_kernel(
    experts, capacity, route_ref, gate_ref, act_ref, grad_ref, gain_ref, pack_ref, *outs
):
    mine, core = my_place()
    width = act_ref.shape[1]
    target = slot_rows(route_ref, mine, experts, capacity)
    widened = act_ref[...].astype(jnp.float32)
    normed = (widened * inverse_rms(widened) * gain_ref[...]).astype(jnp.bfloat16)
    weighted = (to_column(gate_ref[...]) * grad_ref[...].astype(jnp.float32)).astype(jnp.bfloat16)
    for r in range(experts):
        chooser = choose(target, r * capacity, capacity).astype(jnp.bfloat16)
        if r == 0:
            put_halves(outs[0], 0, core, chooser, normed)
            put_halves(outs[1], 0, core, chooser, weighted)
        else:
            put_halves(outs[r + 1], 0, core, chooser, normed)
            put_halves(outs[r + 1], width, core, chooser, weighted)
    pack_ref[:, :width] = act_ref[...]
    pack_ref[:, width : 2 * width] = grad_ref[...]
    lanes = pack_ref.shape[1] - 2 * width
    packed = token_slots(target, experts * capacity, lanes)
    pack_ref[:, 2 * width :] = packed.astype(jnp.float32).astype(jnp.bfloat16)


def join_kernel(*refs):
    *parts, out_ref = refs
    start = 0
    for part in parts:
        out_ref[:, start : start + part.shape[1]] = part[...]
        start += part.shape[1]


def collected(chooser, core, back, capacity, k):
    half = back[0].shape[1] // 2
    start = pl.multiple_of(half * (core if k == 0 else 1 - core), 128)
    columns = pl.ds(start, half)
    first = chooser[:, :capacity]
    total = dot(first, back[0][:, columns]) + dot(first, back[1][:, columns])
    for r, part in enumerate(back[2:], 1):
        total = total + dot(chooser[:, r * capacity : (r + 1) * capacity], part[:, columns])
    return total


def finish_kernel(experts, capacity, pack_ref, *rest):
    *back, out_ref = rest
    core = my_place()[1]
    width = out_ref.shape[1]
    half = width // 2
    slots = experts * capacity
    packed = pack_ref[:, width:]
    parts = packed[:, slots : slots + 3].astype(jnp.float32)
    weight = parts[:, 0:1] + parts[:, 1:2] + parts[:, 2:3]
    for k in range(2):
        columns = slice(k * half, (k + 1) * half)
        mixed = collected(packed, core, back, capacity, k)
        out_ref[:, columns] = (
            pack_ref[:, columns].astype(jnp.float32) + weight * mixed
        ).astype(jnp.bfloat16)


def finish_back_kernel(experts, capacity, pack_ref, *rest):
    *back, out_ref = rest
    core = my_place()[1]
    width = out_ref.shape[1]
    half = width // 2
    packed = pack_ref[:, 2 * width :]
    scaled = [collected(packed, core, back, capacity, k) for k in range(2)]
    widened = [pack_ref[:, k * half : (k + 1) * half].astype(jnp.float32) for k in range(2)]
    squares = sum(jnp.sum(w * w, axis=-1, keepdims=True) for w in widened)
    inverse = lax.rsqrt(squares / width + 1e-06)
    inner = sum(jnp.sum(s * w, axis=-1, keepdims=True) for s, w in zip(scaled, widened))
    factor = inverse * inverse * inverse * (inner / width)
    for k in range(2):
        seed = pack_ref[:, width + k * half : width + (k + 1) * half].astype(jnp.float32)
        out_ref[:, k * half : (k + 1) * half] = (
            seed + scaled[k] * inverse - widened[k] * factor
        ).astype(jnp.bfloat16)


def up_rows(block, half, begin, end):
    large, small, _ = block
    cut = large.shape[0] - half
    return large[half + begin : half + end] if begin < cut else small[begin - cut : end - cut]


def row_ranges(blocks, half):
    cut = max(block[0].shape[0] - half for block in blocks)
    return ((0, cut), (cut, half)) if cut else ((0, half),)


def activations(x_ref, blocks):
    half = x_ref.shape[1] // 2
    pre, upper = 0.0, 0.0
    for k, block in enumerate(blocks):
        first = k * half
        pre = pre + dot(x_ref[:, first : first + half], block[0][:half])
        for begin, end in row_ranges(blocks, half):
            columns = slice(first + begin, first + end)
            upper = upper + dot(x_ref[:, columns], up_rows(block, half, begin, end))
    return pre, upper


def stack_rows(out_ref, pieces):
    width = out_ref.shape[1]
    step = width // 4
    for first in range(0, width, step):
        parts = [ref[:, at + first : at + first + step].astype(jnp.float32) for ref, at in pieces]
        out_ref[:, first : first + step] = jnp.concatenate(parts, axis=0).astype(jnp.bfloat16)


def forward_near_kernel(experts, *refs):
    *near, pair_ref = refs[: experts + 2]
    blocks = refs[experts + 2 : experts + 5], refs[experts + 5 : experts + 8]
    x_ref, part_ref = refs[experts + 8 :]
    pieces = [(ref, 0) for ref in near]
    stack_rows(x_ref, pieces + [(pair_ref, r * x_ref.shape[1]) for r in range(experts - 1)])
    pre, upper = activations(x_ref, blocks)
    hidden = (jax.nn.silu(pre) * upper).astype(jnp.bfloat16)
    half = x_ref.shape[1] // 2
    for k in range(2):
        part_ref[:, k * half : (k + 1) * half] = dot(hidden, blocks[k][2][...])


def put_rows(capacity, total, first, own_ref, near_ref, cross_ref, far_ref):
    columns = slice(first, first + total.shape[1])
    count = total.shape[0] // 2
    own_ref[:, columns] = total[:capacity].astype(jnp.bfloat16)
    far_ref[:, columns] = total[capacity:count]
    near_ref[:, columns] = total[count : count + capacity].astype(jnp.bfloat16)
    cross_ref[:, columns] = total[count + capacity :].astype(jnp.bfloat16)


def forward_side_kernel(capacity, x_ref, part_ref, *refs):
    blocks, outs = (refs[:3], refs[3:6]), refs[6:]
    pre, upper = activations(x_ref, blocks)
    hidden = (jax.nn.silu(pre) * upper).astype(jnp.bfloat16)
    half = x_ref.shape[1] // 2
    for k in range(2):
        total = part_ref[:, k * half : (k + 1) * half] + dot(hidden, blocks[k][2][...])
        put_rows(capacity, total, k * half, *outs)


def backward_kernel(experts, capacity, *refs):
    core = my_place()[1]
    first_ref, grad_ref, *far_refs = refs[: experts + 1]
    pair_ref, rest_ref, gain_ref = refs[experts + 1 : experts + 4]
    blocks = refs[experts + 4 : experts + 16]
    *outs, x_ref, g_ref = refs[experts + 16 :]
    sets = [(blocks[i : i + 3], blocks[i + 3 : i + 6]) for i in (0, 6)]
    width = first_ref.shape[1]
    half = width // 2
    ahead = [(ref, 0) for ref in (first_ref, *far_refs)] + [(pair_ref, pair_ref.shape[1] - width)]
    stack_rows(x_ref, ahead + [(rest_ref, (2 * r - 1) * width) for r in range(1, experts)])
    behind = [(grad_ref, 0)] + [(ref, width) for ref in far_refs] + [(rest_ref, 0)]
    stack_rows(g_ref, behind + [(rest_ref, 2 * r * width) for r in range(1, experts)])
    steps = []
    for blocks in sets:
        pre, upper = activations(x_ref, blocks)
        d_hidden = sum(
            dot_t(g_ref[:, k * half : (k + 1) * half], blocks[k][2][...]) for k in range(2)
        )
        logistic = jax.nn.sigmoid(pre)
        d_gate = d_hidden * upper * logistic * (1.0 + pre * (1.0 - logistic))
        d_up = d_hidden * pre * logistic
        steps.append((d_gate.astype(jnp.bfloat16), d_up.astype(jnp.bfloat16)))
    for k in range(2):
        for begin, end in row_ranges(sets[1], half):
            total = 0.0
            for (d_gate, d_up), blocks in zip(steps, sets):
                upper = up_rows(blocks[k], half, begin, end)
                total = total + dot_t(d_gate, blocks[k][0][begin:end]) + dot_t(d_up, upper)
            start = half * (core if k == 0 else 1 - core) + begin
            gain = gain_ref[:, pl.ds(pl.multiple_of(start, 128), end - begin)]
            put_rows(capacity, gain * total, k * half + begin, *outs)


def send_sums(far, received, experts, capacity, step):
    sums = []
    for r in range(1, experts):
        rows = slice((r - 1) * capacity, r * capacity)
        summed = (far[rows] + received[rows].astype(jnp.float32)).astype(jnp.bfloat16)
        sums.append(to_section(summed, step, lambda i, r=r: i - SLICES * r))
    return sums


def body(
    fwd_act,
    fwd_route,
    fwd_gate,
    bwd_act,
    bwd_grad,
    bwd_route,
    bwd_gate,
    norm_gain,
    w_gate,
    w_up,
    w_down,
):
    experts = lax.axis_size("ep") // SLICES
    tokens, width = fwd_act.shape[1:]
    capacity = 2 * ((5 * tokens + 8 * experts - 1) // (8 * experts))
    shifts = range(1, experts)
    gate, up, down = w_gate[0, 0], w_up[0, 0], w_down[0, 0]
    row = (1, tokens)
    lanes = -(-(experts * capacity + 3) // 128) * 128
    slots = ((capacity, width), jnp.bfloat16)
    two_slots = ((capacity, 2 * width), jnp.bfloat16)

    large, small = split_weights(gate, up)
    side_down = swap(down, SIDE)
    near_down = swap(down, NEAR)
    fwd_pack, *fwd_groups = call_fetching(
        functools.partial(prepare_kernel, experts, capacity),
        "prepare",
        [((tokens, width + lanes), jnp.bfloat16)] + [slots] * experts,
        LONG,
        (fwd_route.reshape(row), fwd_gate.reshape(row), fwd_act[0], norm_gain),
    )
    fwd_far = [to_expert(fwd_groups[r], r) for r in shifts]
    first_pair = swap(fwd_groups[0], FAR)
    fwd_pack = to_section(fwd_pack, 1)
    bwd_pack, bwd_first, grad_first, *bwd_groups = call(
        functools.partial(prepare_back_kernel, experts, capacity),
        "prepare_back",
        [((tokens, 2 * width + lanes), jnp.bfloat16), slots, slots] + [two_slots] * (experts - 1),
        SHORT,
        (bwd_route.reshape(row), bwd_gate.reshape(row), bwd_act[0], bwd_grad[0], norm_gain),
        held=8,
    )

    first = (side_down, near_down, fwd_pack, first_pair, bwd_first, large, *fwd_far)
    bwd_pack = to_section(after(bwd_pack, *first), -1)
    near_up = swap(after(up, *first), NEAR)
    (mixed,) = call(
        join_kernel,
        "join",
        [((capacity, experts * width), jnp.bfloat16)],
        SHORT,
        (*after(tuple(fwd_far), *first), bwd_first),
    )
    own_pair = swap(mixed, FAR)
    side_large = swap(after(large, *first), SIDE)
    bwd_far = [to_expert(after(bwd_groups[r - 1], *first), r) for r in shifts]

    (rest,) = call(
        join_kernel,
        "join_back",
        [((capacity, (2 * experts - 1) * width), jnp.bfloat16)],
        LONG,
        (after(grad_first, side_large), *bwd_far),
    )
    second = (rest, bwd_pack, near_up, own_pair)
    rest_pair = swap(rest, FAR)
    near_gate = swap(after(gate, *second), NEAR)
    side_small = swap(after(small, *second), SIDE)
    side_near_large = swap(after(side_large, *second), NEAR)
    side_near_down = swap(after(side_down, *second), NEAR)
    mine = ((gate, up, down), (near_gate, near_up, near_down))

    rows = (2 * experts * capacity, width)
    far = ((experts - 1) * capacity, width)
    outs = [slots, slots, (far, jnp.bfloat16), (far, jnp.float32)]
    pieces = after((fwd_groups[0], *fwd_far, first_pair, own_pair), rest, side_near_down)
    fwd_x, part = call(
        functools.partial(forward_near_kernel, experts),
        "forward_near",
        [(rows, jnp.bfloat16), (rows, jnp.float32)],
        SHORT,
        (*pieces, *mine[0], *mine[1]),
        held=6,
    )
    side_near_small = swap(after(side_small, part, side_near_large), NEAR)
    beside = ((side_large, side_small, side_down), (side_near_large, side_near_small, side_near_down))
    fwd_own, fwd_near, fwd_cross, fwd_sum = call(
        functools.partial(forward_side_kernel, capacity),
        "forward_side",
        outs,
        SHORT,
        (fwd_x, part, *beside[0], *beside[1]),
        held=6,
    )
    rest_pair = after(rest_pair, fwd_own)
    fwd_received = swap(fwd_cross, FAR)
    fwd_near_sums = to_section(fwd_own, 1)
    fwd_second = to_section(fwd_near, 1, lambda i: i ^ FAR)

    bwd_own, bwd_near, bwd_cross, bwd_sum = call(
        functools.partial(backward_kernel, experts, capacity),
        "backward",
        outs,
        SHORT,
        (bwd_first, grad_first, *bwd_far, own_pair, rest_pair, norm_gain)
        + (*mine[0], *mine[1], *beside[0], *beside[1]),
        held=14,
        scratch=(pltpu.VMEM(rows, jnp.bfloat16),) * 2,
    )
    bwd_received = swap(after(bwd_cross, fwd_received, fwd_near_sums), FAR)
    fwd_sums = send_sums(fwd_sum, fwd_received, experts, capacity, 1)
    bwd_near_sums = to_section(after(bwd_own, fwd_received), -1)
    bwd_sums = send_sums(bwd_sum, bwd_received, experts, capacity, -1)
    both = (fwd_received, bwd_received)
    bwd_second = to_section(after(bwd_near, *both), -1, lambda i: i ^ FAR)
    fwd_back = (fwd_near_sums, fwd_second, *fwd_sums)
    bwd_back = (bwd_near_sums, bwd_second, *bwd_sums)

    (fwd_next,) = call(
        functools.partial(finish_kernel, experts, capacity),
        "finish",
        [((tokens, width), jnp.bfloat16)],
        SHORT,
        (fwd_pack, *fwd_back),
        held=8,
    )
    (held_pack,) = call(
        join_kernel,
        "hold",
        [(bwd_pack.shape, jnp.bfloat16)],
        SHORT,
        (after(bwd_pack, bwd_received),),
    )
    (bwd_next,) = call(
        functools.partial(finish_back_kernel, experts, capacity),
        "finish_back",
        [((tokens, width), jnp.bfloat16)],
        SHORT,
        (held_pack, *bwd_back),
        held=8,
    )
    return (fwd_next[None], bwd_next[None])


def solution(mesh):
    rows = P("pp", "ep", None)
    weights = P("pp", "ep", None, None)
    in_specs = (rows,) * 7 + (P("pp", None),) + (weights,) * 3
    return jax.shard_map(
        body, mesh=mesh, in_specs=in_specs, out_specs=(rows, rows), check_vma=False
    )
```

```python
import functools

import jax
import jax.numpy as jnp
from jax import lax
from jax.experimental import pallas as pl
from jax.experimental.pallas import tpu as pltpu
from jax.sharding import PartitionSpec as P

SLICES = 8
NEAR, SIDE, FAR = 1, 2, 4
SHORT, LONG = 10**6, 2 * 10**11
FULL = 58 * 2**20


def swap(value, bit):
    return lax.ppermute(value, "ep", [(i, i ^ bit) for i in range(lax.axis_size("ep"))])


def to_expert(value, shift):
    count = lax.axis_size("ep")
    return lax.ppermute(value, "ep", [(i, (i + SLICES * shift) % count) for i in range(count)])


def to_section(value, step, place=lambda i: i):
    sections, count = lax.axis_size("pp"), lax.axis_size("ep")
    pairs = [
        (p * count + i, (p + step) % sections * count + place(i) % count)
        for p in range(sections)
        for i in range(count)
    ]
    return lax.ppermute(value, ("pp", "ep"), pairs)


def after(value, *done):
    return lax.optimization_barrier((value, done))[0]


def dot(a, b):
    return jnp.dot(a, b, preferred_element_type=jnp.float32)


def dot_t(a, b):
    return lax.dot_general(a, b, (((1,), (1,)), ((), ())), preferred_element_type=jnp.float32)


def dot_first(a, b):
    return lax.dot_general(a, b, (((0,), (0,)), ((), ())), preferred_element_type=jnp.float32)


def call(kernel, name, outs, cost, args, held=4, scratch=()):
    space = pl.BlockSpec(memory_space=pltpu.VMEM)
    return pl.pallas_call(
        kernel,
        name=name,
        out_shape=[jax.ShapeDtypeStruct(shape, kind) for shape, kind in outs],
        in_specs=[space] * len(args),
        out_specs=[space] * len(outs),
        scratch_shapes=list(scratch),
        cost_estimate=pl.CostEstimate(flops=cost, bytes_accessed=0, transcendentals=0),
        compiler_params=pltpu.CompilerParams(vmem_limit_bytes=held * 2**20),
    )(*args)


def call_fetching(kernel, name, outs, cost, args):
    count = len(args)

    def fetching(*refs):
        sources, rest = refs[:count], refs[count : count + len(outs)]
        held, sems = refs[count + len(outs) : -1], refs[-1]
        copies = [
            pltpu.make_async_copy(source, target, sems.at[i])
            for i, (source, target) in enumerate(zip(sources, held))
        ]
        for copy in copies:
            copy.start()
        for copy in copies:
            copy.wait()
        kernel(*held, *rest)

    return pl.pallas_call(
        fetching,
        name=name,
        out_shape=[jax.ShapeDtypeStruct(shape, kind) for shape, kind in outs],
        in_specs=[pl.BlockSpec(memory_space=pltpu.HBM)] * count,
        out_specs=[pl.BlockSpec(memory_space=pltpu.VMEM)] * len(outs),
        scratch_shapes=[pltpu.VMEM(arg.shape, arg.dtype) for arg in args]
        + [pltpu.SemaphoreType.DMA((count,))],
        cost_estimate=pl.CostEstimate(flops=cost, bytes_accessed=0, transcendentals=0),
        compiler_params=pltpu.CompilerParams(vmem_limit_bytes=FULL),
    )(*args)


def my_place():
    me = lax.axis_index("ep")
    return me // SLICES, me % 2


def split_kernel(gate_ref, up_ref, large_ref, small_ref, sems):
    half, cut = gate_ref.shape[0], up_ref.shape[0] - small_ref.shape[0]
    copies = [
        pltpu.make_async_copy(gate_ref, large_ref.at[pl.ds(0, half)], sems.at[0]),
        pltpu.make_async_copy(up_ref.at[pl.ds(0, cut)], large_ref.at[pl.ds(half, cut)], sems.at[1]),
        pltpu.make_async_copy(up_ref.at[pl.ds(cut, half - cut)], small_ref, sems.at[2]),
    ]
    for copy in copies:
        copy.start()
    for copy in copies:
        copy.wait()


def split_weights(gate, up):
    half, units = up.shape
    cut = half * 3 // 7 // 128 * 128
    anywhere = pl.BlockSpec(memory_space=pl.ANY)
    return pl.pallas_call(
        split_kernel,
        name="split_weights",
        out_shape=[
            jax.ShapeDtypeStruct((half + cut, units), up.dtype),
            jax.ShapeDtypeStruct((half - cut, units), up.dtype),
        ],
        in_specs=[anywhere] * 2,
        out_specs=[anywhere] * 2,
        scratch_shapes=[pltpu.SemaphoreType.DMA((3,))],
        cost_estimate=pl.CostEstimate(flops=SHORT, bytes_accessed=0, transcendentals=0),
        compiler_params=pltpu.CompilerParams(vmem_limit_bytes=2 * 2**20),
    )(gate, up)


def slot_rows(route_ref, mine, experts, capacity):
    chosen = route_ref[...]
    tokens = chosen.shape[1]
    onehot = lax.broadcasted_iota(jnp.int32, (experts, tokens), 0) == chosen
    before = lax.broadcasted_iota(jnp.int32, (tokens, tokens), 0) <= lax.broadcasted_iota(
        jnp.int32, (tokens, tokens), 1
    )
    running = dot(onehot.astype(jnp.bfloat16), before.astype(jnp.bfloat16))
    position = jnp.sum(jnp.where(onehot, running, 0.0), axis=0, keepdims=True) - 1.0
    relative = chosen - mine
    relative = jnp.where(relative < 0, relative + experts, relative)
    return relative * capacity + position.astype(jnp.int32)


def choose(target, first, count):
    slots = lax.broadcasted_iota(jnp.int32, (count, target.shape[1]), 0)
    return slots == target - first


def to_column(row):
    size = row.shape[1]
    same = lax.broadcasted_iota(jnp.int32, (size, size), 0) == lax.broadcasted_iota(
        jnp.int32, (size, size), 1
    )
    return jnp.sum(jnp.where(same, row, 0.0), axis=1, keepdims=True)


def inverse_rms(widened):
    return lax.rsqrt(jnp.mean(widened * widened, axis=-1, keepdims=True) + 1e-06)


def put_halves(out_ref, first, core, chooser, rows):
    half = rows.shape[1] // 2
    for k in range(2):
        placed = dot(chooser, rows[:, k * half : (k + 1) * half]).astype(jnp.bfloat16)
        start = first + half * (core if k == 0 else 1 - core)
        out_ref[:, pl.ds(pl.multiple_of(start, 128), half)] = placed


def token_slots(target, count, lanes):
    column = to_column(target.astype(jnp.float32)).astype(jnp.int32)
    return lax.broadcasted_iota(jnp.int32, (target.shape[1], lanes), 1) == column


def prepare_kernel(experts, capacity, route_ref, gate_ref, act_ref, gain_ref, pack_ref, *outs):
    mine, core = my_place()
    width = act_ref.shape[1]
    target = slot_rows(route_ref, mine, experts, capacity)
    widened = act_ref[...].astype(jnp.float32)
    normed = (widened * inverse_rms(widened) * gain_ref[...]).astype(jnp.bfloat16)
    for r in range(experts):
        chooser = choose(target, r * capacity, capacity).astype(jnp.bfloat16)
        put_halves(outs[r], 0, core, chooser, normed)
    pack_ref[:, :width] = act_ref[...]
    lanes = pack_ref.shape[1] - width
    slots = experts * capacity
    packed = token_slots(target, slots, lanes).astype(jnp.float32)
    rest = to_column(gate_ref[...])
    lane = lax.broadcasted_iota(jnp.int32, packed.shape, 1)
    for part in range(3):
        piece = rest.astype(jnp.bfloat16).astype(jnp.float32)
        packed = jnp.where(lane == slots + part, piece, packed)
        rest = rest - piece
    pack_ref[:, width:] = packed.astype(jnp.bfloat16)


def prepare_back_kernel(
    experts, capacity, route_ref, gate_ref, act_ref, grad_ref, gain_ref, pack_ref, *outs
):
    mine, core = my_place()
    width = act_ref.shape[1]
    target = slot_rows(route_ref, mine, experts, capacity)
    widened = act_ref[...].astype(jnp.float32)
    normed = (widened * inverse_rms(widened) * gain_ref[...]).astype(jnp.bfloat16)
    weighted = (to_column(gate_ref[...]) * grad_ref[...].astype(jnp.float32)).astype(jnp.bfloat16)
    for r in range(experts):
        chooser = choose(target, r * capacity, capacity).astype(jnp.bfloat16)
        if r == 0:
            put_halves(outs[0], 0, core, chooser, normed)
            put_halves(outs[1], 0, core, chooser, weighted)
        else:
            put_halves(outs[r + 1], 0, core, chooser, normed)
            put_halves(outs[r + 1], width, core, chooser, weighted)
    pack_ref[:, :width] = act_ref[...]
    pack_ref[:, width : 2 * width] = grad_ref[...]
    lanes = pack_ref.shape[1] - 2 * width
    packed = token_slots(target, experts * capacity, lanes)
    pack_ref[:, 2 * width :] = packed.astype(jnp.float32).astype(jnp.bfloat16)


def join_kernel(*refs):
    *parts, out_ref = refs
    start = 0
    for part in parts:
        out_ref[:, start : start + part.shape[1]] = part[...]
        start += part.shape[1]


def collected(chooser, core, back, capacity, k):
    half = back[0].shape[1] // 2
    start = pl.multiple_of(half * (core if k == 0 else 1 - core), 128)
    columns = pl.ds(start, half)
    first = chooser[:, :capacity]
    total = dot(first, back[0][:, columns]) + dot(first, back[1][:, columns])
    for r, part in enumerate(back[2:], 1):
        total = total + dot(chooser[:, r * capacity : (r + 1) * capacity], part[:, columns])
    return total


def finish_kernel(experts, capacity, pack_ref, *rest):
    *back, out_ref = rest
    core = my_place()[1]
    width = out_ref.shape[1]
    half = width // 2
    slots = experts * capacity
    packed = pack_ref[:, width:]
    parts = packed[:, slots : slots + 3].astype(jnp.float32)
    weight = parts[:, 0:1] + parts[:, 1:2] + parts[:, 2:3]
    for k in range(2):
        columns = slice(k * half, (k + 1) * half)
        mixed = collected(packed, core, back, capacity, k)
        out_ref[:, columns] = (
            pack_ref[:, columns].astype(jnp.float32) + weight * mixed
        ).astype(jnp.bfloat16)


def finish_back_kernel(experts, capacity, pack_ref, *rest):
    *back, out_ref = rest
    core = my_place()[1]
    width = out_ref.shape[1]
    half = width // 2
    packed = pack_ref[:, 2 * width :]
    scaled = [collected(packed, core, back, capacity, k) for k in range(2)]
    widened = [pack_ref[:, k * half : (k + 1) * half].astype(jnp.float32) for k in range(2)]
    squares = sum(jnp.sum(w * w, axis=-1, keepdims=True) for w in widened)
    inverse = lax.rsqrt(squares / width + 1e-06)
    inner = sum(jnp.sum(s * w, axis=-1, keepdims=True) for s, w in zip(scaled, widened))
    factor = inverse * inverse * inverse * (inner / width)
    for k in range(2):
        seed = pack_ref[:, width + k * half : width + (k + 1) * half].astype(jnp.float32)
        out_ref[:, k * half : (k + 1) * half] = (
            seed + scaled[k] * inverse - widened[k] * factor
        ).astype(jnp.bfloat16)


def up_rows(block, half, begin, end):
    large, small, _ = block
    cut = large.shape[0] - half
    return large[half + begin : half + end] if begin < cut else small[begin - cut : end - cut]


def row_ranges(blocks, half):
    cut = max(block[0].shape[0] - half for block in blocks)
    return ((0, cut), (cut, half)) if cut else ((0, half),)


def activations(x_ref, blocks):
    half = x_ref.shape[1] // 2
    pre, upper = 0.0, 0.0
    for k, block in enumerate(blocks):
        first = k * half
        pre = pre + dot(x_ref[:, first : first + half], block[0][:half])
        for begin, end in row_ranges(blocks, half):
            columns = slice(first + begin, first + end)
            upper = upper + dot(x_ref[:, columns], up_rows(block, half, begin, end))
    return pre, upper


def stack_rows(out_ref, pieces):
    width = out_ref.shape[1]
    step = width // 4
    for first in range(0, width, step):
        parts = [ref[:, at + first : at + first + step].astype(jnp.float32) for ref, at in pieces]
        out_ref[:, first : first + step] = jnp.concatenate(parts, axis=0).astype(jnp.bfloat16)


def forward_near_kernel(experts, *refs):
    *near, pair_ref = refs[: experts + 2]
    blocks = refs[experts + 2 : experts + 5], refs[experts + 5 : experts + 8]
    x_ref, part_ref = refs[experts + 8 :]
    pieces = [(ref, 0) for ref in near]
    stack_rows(x_ref, pieces + [(pair_ref, r * x_ref.shape[1]) for r in range(experts - 1)])
    pre, upper = activations(x_ref, blocks)
    hidden = (jax.nn.silu(pre) * upper).astype(jnp.bfloat16)
    half = x_ref.shape[1] // 2
    for k in range(2):
        part_ref[:, k * half : (k + 1) * half] = dot(hidden, blocks[k][2][...])


def put_rows(capacity, total, first, own_ref, near_ref, cross_ref, far_ref):
    columns = slice(first, first + total.shape[1])
    count = total.shape[0] // 2
    own_ref[:, columns] = total[:capacity].astype(jnp.bfloat16)
    far_ref[:, columns] = total[capacity:count]
    near_ref[:, columns] = total[count : count + capacity].astype(jnp.bfloat16)
    cross_ref[:, columns] = total[count + capacity :].astype(jnp.bfloat16)


def forward_side_kernel(capacity, x_ref, part_ref, *refs):
    blocks, outs = (refs[:3], refs[3:6]), refs[6:]
    pre, upper = activations(x_ref, blocks)
    hidden = (jax.nn.silu(pre) * upper).astype(jnp.bfloat16)
    half = x_ref.shape[1] // 2
    for k in range(2):
        total = part_ref[:, k * half : (k + 1) * half] + dot(hidden, blocks[k][2][...])
        put_rows(capacity, total, k * half, *outs)


def backward_kernel(experts, capacity, *refs):
    core = my_place()[1]
    first_ref, grad_ref, *far_refs = refs[: experts + 1]
    pair_ref, rest_ref, gain_ref = refs[experts + 1 : experts + 4]
    blocks = refs[experts + 4 : experts + 16]
    *outs, x_ref, g_ref = refs[experts + 16 :]
    sets = [(blocks[i : i + 3], blocks[i + 3 : i + 6]) for i in (0, 6)]
    width = first_ref.shape[1]
    half = width // 2
    ahead = [(ref, 0) for ref in (first_ref, *far_refs)] + [(pair_ref, pair_ref.shape[1] - width)]
    stack_rows(x_ref, ahead + [(rest_ref, (2 * r - 1) * width) for r in range(1, experts)])
    behind = [(grad_ref, 0)] + [(ref, width) for ref in far_refs] + [(rest_ref, 0)]
    stack_rows(g_ref, behind + [(rest_ref, 2 * r * width) for r in range(1, experts)])
    steps = []
    for blocks in sets:
        pre, upper = activations(x_ref, blocks)
        d_hidden = sum(
            dot_t(g_ref[:, k * half : (k + 1) * half], blocks[k][2][...]) for k in range(2)
        )
        logistic = jax.nn.sigmoid(pre)
        d_gate = d_hidden * upper * logistic * (1.0 + pre * (1.0 - logistic))
        d_up = d_hidden * pre * logistic
        steps.append((d_gate.astype(jnp.bfloat16), d_up.astype(jnp.bfloat16)))
    for k in range(2):
        for begin, end in row_ranges(sets[1], half):
            total = 0.0
            for (d_gate, d_up), blocks in zip(steps, sets):
                upper = up_rows(blocks[k], half, begin, end)
                total = total + dot_t(d_gate, blocks[k][0][begin:end]) + dot_t(d_up, upper)
            start = half * (core if k == 0 else 1 - core) + begin
            gain = gain_ref[:, pl.ds(pl.multiple_of(start, 128), end - begin)]
            put_rows(capacity, gain * total, k * half + begin, *outs)


def send_sums(far, received, experts, capacity, step):
    sums = []
    for r in range(1, experts):
        rows = slice((r - 1) * capacity, r * capacity)
        summed = (far[rows] + received[rows].astype(jnp.float32)).astype(jnp.bfloat16)
        sums.append(to_section(summed, step, lambda i, r=r: i - SLICES * r))
    return sums


def body(
    fwd_act,
    fwd_route,
    fwd_gate,
    bwd_act,
    bwd_grad,
    bwd_route,
    bwd_gate,
    norm_gain,
    w_gate,
    w_up,
    w_down,
):
    experts = lax.axis_size("ep") // SLICES
    tokens, width = fwd_act.shape[1:]
    capacity = 2 * ((5 * tokens + 8 * experts - 1) // (8 * experts))
    shifts = range(1, experts)
    gate, up, down = w_gate[0, 0], w_up[0, 0], w_down[0, 0]
    row = (1, tokens)
    lanes = -(-(experts * capacity + 3) // 128) * 128
    slots = ((capacity, width), jnp.bfloat16)
    two_slots = ((capacity, 2 * width), jnp.bfloat16)

    large, small = split_weights(gate, up)
    side_down = swap(down, SIDE)
    fwd_pack, *fwd_groups = call_fetching(
        functools.partial(prepare_kernel, experts, capacity),
        "prepare",
        [((tokens, width + lanes), jnp.bfloat16)] + [slots] * experts,
        LONG,
        (fwd_route.reshape(row), fwd_gate.reshape(row), fwd_act[0], norm_gain),
    )
    fwd_far = [to_expert(fwd_groups[r], r) for r in shifts]
    first_pair = swap(fwd_groups[0], FAR)
    near_down = swap(after(down, fwd_groups[0]), NEAR)
    fwd_pack = to_section(fwd_pack, 1)
    bwd_pack, bwd_first, grad_first, *bwd_groups = call(
        functools.partial(prepare_back_kernel, experts, capacity),
        "prepare_back",
        [((tokens, 2 * width + lanes), jnp.bfloat16), slots, slots] + [two_slots] * (experts - 1),
        SHORT,
        (bwd_route.reshape(row), bwd_gate.reshape(row), bwd_act[0], bwd_grad[0], norm_gain),
        held=8,
    )

    first = (side_down, near_down, fwd_pack, first_pair, bwd_first, large, *fwd_far)
    bwd_pack = to_section(after(bwd_pack, *first), -1)
    near_up = swap(after(up, *first), NEAR)
    (mixed,) = call(
        join_kernel,
        "join",
        [((capacity, experts * width), jnp.bfloat16)],
        SHORT,
        (*after(tuple(fwd_far), *first), bwd_first),
    )
    own_pair = swap(mixed, FAR)
    side_large = swap(after(large, *first), SIDE)
    bwd_far = [to_expert(after(bwd_groups[r - 1], *first), r) for r in shifts]

    (rest,) = call(
        join_kernel,
        "join_back",
        [((capacity, (2 * experts - 1) * width), jnp.bfloat16)],
        LONG,
        (after(grad_first, side_large), *bwd_far),
    )
    second = (rest, bwd_pack, near_up, own_pair)
    rest_pair = swap(rest, FAR)
    near_gate = swap(after(gate, *second), NEAR)
    side_small = swap(after(small, *second), SIDE)
    side_near_large = swap(after(side_large, *second), NEAR)
    side_near_down = swap(after(side_down, *second), NEAR)
    mine = ((gate, up, down), (near_gate, near_up, near_down))

    rows = (2 * experts * capacity, width)
    far = ((experts - 1) * capacity, width)
    outs = [slots, slots, (far, jnp.bfloat16), (far, jnp.float32)]
    pieces = after((fwd_groups[0], *fwd_far, first_pair, own_pair), rest, side_near_down)
    fwd_x, part = call(
        functools.partial(forward_near_kernel, experts),
        "forward_near",
        [(rows, jnp.bfloat16), (rows, jnp.float32)],
        SHORT,
        (*pieces, *mine[0], *mine[1]),
        held=6,
    )
    side_near_small = swap(after(side_small, part, side_near_large), NEAR)
    beside = ((side_large, side_small, side_down), (side_near_large, side_near_small, side_near_down))
    fwd_own, fwd_near, fwd_cross, fwd_sum = call(
        functools.partial(forward_side_kernel, capacity),
        "forward_side",
        outs,
        SHORT,
        (fwd_x, part, *beside[0], *beside[1]),
        held=6,
    )
    rest_pair = after(rest_pair, fwd_own)
    fwd_received = swap(fwd_cross, FAR)
    fwd_second = to_section(fwd_near, 1, lambda i: i ^ FAR)
    fwd_near_sums = to_section(fwd_own, 1)

    bwd_own, bwd_near, bwd_cross, bwd_sum = call(
        functools.partial(backward_kernel, experts, capacity),
        "backward",
        outs,
        SHORT,
        (bwd_first, grad_first, *bwd_far, own_pair, rest_pair, norm_gain)
        + (*mine[0], *mine[1], *beside[0], *beside[1]),
        held=14,
        scratch=(pltpu.VMEM(rows, jnp.bfloat16),) * 2,
    )
    bwd_received = swap(after(bwd_cross, fwd_received), FAR)
    fwd_sums = send_sums(fwd_sum, fwd_received, experts, capacity, 1)
    bwd_near_sums = to_section(after(bwd_own, fwd_received), -1)
    bwd_sums = send_sums(bwd_sum, bwd_received, experts, capacity, -1)
    both = (fwd_received, bwd_received)
    bwd_second = to_section(after(bwd_near, *both), -1, lambda i: i ^ FAR)
    fwd_back = (fwd_near_sums, fwd_second, *fwd_sums)
    bwd_back = (bwd_near_sums, bwd_second, *bwd_sums)

    (fwd_next,) = call(
        functools.partial(finish_kernel, experts, capacity),
        "finish",
        [((tokens, width), jnp.bfloat16)],
        SHORT,
        (fwd_pack, *fwd_back),
        held=8,
    )
    (held_pack,) = call(
        join_kernel,
        "hold",
        [(bwd_pack.shape, jnp.bfloat16)],
        SHORT,
        (after(bwd_pack, bwd_received),),
    )
    (bwd_next,) = call(
        functools.partial(finish_back_kernel, experts, capacity),
        "finish_back",
        [((tokens, width), jnp.bfloat16)],
        SHORT,
        (held_pack, *bwd_back),
        held=8,
    )
    return (fwd_next[None], bwd_next[None])


def solution(mesh):
    rows = P("pp", "ep", None)
    weights = P("pp", "ep", None, None)
    in_specs = (rows,) * 7 + (P("pp", None),) + (weights,) * 3
    return jax.shard_map(
        body, mesh=mesh, in_specs=in_specs, out_specs=(rows, rows), check_vma=False
    )
```

```python
import functools

import jax
import jax.numpy as jnp
from jax import lax
from jax.experimental import pallas as pl
from jax.experimental.pallas import tpu as pltpu
from jax.sharding import PartitionSpec as P

SLICES = 8
NEAR, SIDE, FAR = 1, 2, 4
SHORT, LONG = 10**6, 2 * 10**11
FULL = 58 * 2**20


def swap(value, bit):
    return lax.ppermute(value, "ep", [(i, i ^ bit) for i in range(lax.axis_size("ep"))])


def to_expert(value, shift):
    count = lax.axis_size("ep")
    return lax.ppermute(value, "ep", [(i, (i + SLICES * shift) % count) for i in range(count)])


def to_section(value, step, place=lambda i: i):
    sections, count = lax.axis_size("pp"), lax.axis_size("ep")
    pairs = [
        (p * count + i, (p + step) % sections * count + place(i) % count)
        for p in range(sections)
        for i in range(count)
    ]
    return lax.ppermute(value, ("pp", "ep"), pairs)


def after(value, *done):
    return lax.optimization_barrier((value, done))[0]


def dot(a, b):
    return jnp.dot(a, b, preferred_element_type=jnp.float32)


def dot_t(a, b):
    return lax.dot_general(a, b, (((1,), (1,)), ((), ())), preferred_element_type=jnp.float32)


def dot_first(a, b):
    return lax.dot_general(a, b, (((0,), (0,)), ((), ())), preferred_element_type=jnp.float32)


def call(kernel, name, outs, cost, args, held=1, scratch=()):
    space = pl.BlockSpec(memory_space=pltpu.VMEM)
    return pl.pallas_call(
        kernel,
        name=name,
        out_shape=[jax.ShapeDtypeStruct(shape, kind) for shape, kind in outs],
        in_specs=[space] * len(args),
        out_specs=[space] * len(outs),
        scratch_shapes=list(scratch),
        cost_estimate=pl.CostEstimate(flops=cost, bytes_accessed=0, transcendentals=0),
        compiler_params=pltpu.CompilerParams(vmem_limit_bytes=held * 2**20),
    )(*args)


def call_fetching(kernel, name, outs, cost, args):
    count = len(args)

    def fetching(*refs):
        sources, rest = refs[:count], refs[count : count + len(outs)]
        held, sems = refs[count + len(outs) : -1], refs[-1]
        copies = [
            pltpu.make_async_copy(source, target, sems.at[i])
            for i, (source, target) in enumerate(zip(sources, held))
        ]
        for copy in copies:
            copy.start()
        for copy in copies:
            copy.wait()
        kernel(*held, *rest)

    return pl.pallas_call(
        fetching,
        name=name,
        out_shape=[jax.ShapeDtypeStruct(shape, kind) for shape, kind in outs],
        in_specs=[pl.BlockSpec(memory_space=pltpu.HBM)] * count,
        out_specs=[pl.BlockSpec(memory_space=pltpu.VMEM)] * len(outs),
        scratch_shapes=[pltpu.VMEM(arg.shape, arg.dtype) for arg in args]
        + [pltpu.SemaphoreType.DMA((count,))],
        cost_estimate=pl.CostEstimate(flops=cost, bytes_accessed=0, transcendentals=0),
        compiler_params=pltpu.CompilerParams(vmem_limit_bytes=FULL),
    )(*args)


def my_place():
    me = lax.axis_index("ep")
    return me // SLICES, me % 2


def split_kernel(gate_ref, up_ref, large_ref, small_ref, sems):
    half, cut = gate_ref.shape[0], up_ref.shape[0] - small_ref.shape[0]
    copies = [
        pltpu.make_async_copy(gate_ref, large_ref.at[pl.ds(0, half)], sems.at[0]),
        pltpu.make_async_copy(up_ref.at[pl.ds(0, cut)], large_ref.at[pl.ds(half, cut)], sems.at[1]),
        pltpu.make_async_copy(up_ref.at[pl.ds(cut, half - cut)], small_ref, sems.at[2]),
    ]
    for copy in copies:
        copy.start()
    for copy in copies:
        copy.wait()


def split_weights(gate, up):
    half, units = up.shape
    cut = half * 3 // 7 // 128 * 128
    anywhere = pl.BlockSpec(memory_space=pl.ANY)
    return pl.pallas_call(
        split_kernel,
        name="split_weights",
        out_shape=[
            jax.ShapeDtypeStruct((half + cut, units), up.dtype),
            jax.ShapeDtypeStruct((half - cut, units), up.dtype),
        ],
        in_specs=[anywhere] * 2,
        out_specs=[anywhere] * 2,
        scratch_shapes=[pltpu.SemaphoreType.DMA((3,))],
        cost_estimate=pl.CostEstimate(flops=SHORT, bytes_accessed=0, transcendentals=0),
        compiler_params=pltpu.CompilerParams(vmem_limit_bytes=2 * 2**20),
    )(gate, up)


def slot_rows(route_ref, mine, experts, capacity):
    chosen = route_ref[...]
    tokens = chosen.shape[1]
    onehot = lax.broadcasted_iota(jnp.int32, (experts, tokens), 0) == chosen
    before = lax.broadcasted_iota(jnp.int32, (tokens, tokens), 0) <= lax.broadcasted_iota(
        jnp.int32, (tokens, tokens), 1
    )
    running = dot(onehot.astype(jnp.bfloat16), before.astype(jnp.bfloat16))
    position = jnp.sum(jnp.where(onehot, running, 0.0), axis=0, keepdims=True) - 1.0
    relative = chosen - mine
    relative = jnp.where(relative < 0, relative + experts, relative)
    return relative * capacity + position.astype(jnp.int32)


def choose(target, first, count):
    slots = lax.broadcasted_iota(jnp.int32, (count, target.shape[1]), 0)
    return slots == target - first


def to_column(row):
    size = row.shape[1]
    same = lax.broadcasted_iota(jnp.int32, (size, size), 0) == lax.broadcasted_iota(
        jnp.int32, (size, size), 1
    )
    return jnp.sum(jnp.where(same, row, 0.0), axis=1, keepdims=True)


def inverse_rms(widened):
    return lax.rsqrt(jnp.mean(widened * widened, axis=-1, keepdims=True) + 1e-06)


def put_halves(out_ref, first, core, chooser, rows):
    half = rows.shape[1] // 2
    for k in range(2):
        placed = dot(chooser, rows[:, k * half : (k + 1) * half]).astype(jnp.bfloat16)
        start = first + half * (core if k == 0 else 1 - core)
        out_ref[:, pl.ds(pl.multiple_of(start, 128), half)] = placed


def token_slots(target, count, lanes):
    column = to_column(target.astype(jnp.float32)).astype(jnp.int32)
    return lax.broadcasted_iota(jnp.int32, (target.shape[1], lanes), 1) == column


def prepare_kernel(experts, capacity, route_ref, gate_ref, act_ref, gain_ref, pack_ref, *outs):
    mine, core = my_place()
    width = act_ref.shape[1]
    target = slot_rows(route_ref, mine, experts, capacity)
    widened = act_ref[...].astype(jnp.float32)
    normed = (widened * inverse_rms(widened) * gain_ref[...]).astype(jnp.bfloat16)
    for r in range(experts):
        chooser = choose(target, r * capacity, capacity).astype(jnp.bfloat16)
        put_halves(outs[r], 0, core, chooser, normed)
    pack_ref[:, :width] = act_ref[...]
    lanes = pack_ref.shape[1] - width
    slots = experts * capacity
    packed = token_slots(target, slots, lanes).astype(jnp.float32)
    rest = to_column(gate_ref[...])
    lane = lax.broadcasted_iota(jnp.int32, packed.shape, 1)
    for part in range(3):
        piece = rest.astype(jnp.bfloat16).astype(jnp.float32)
        packed = jnp.where(lane == slots + part, piece, packed)
        rest = rest - piece
    pack_ref[:, width:] = packed.astype(jnp.bfloat16)


def prepare_back_kernel(
    experts, capacity, route_ref, gate_ref, act_ref, grad_ref, gain_ref, pack_ref, *outs
):
    mine, core = my_place()
    width = act_ref.shape[1]
    target = slot_rows(route_ref, mine, experts, capacity)
    widened = act_ref[...].astype(jnp.float32)
    normed = (widened * inverse_rms(widened) * gain_ref[...]).astype(jnp.bfloat16)
    weighted = (to_column(gate_ref[...]) * grad_ref[...].astype(jnp.float32)).astype(jnp.bfloat16)
    for r in range(experts):
        chooser = choose(target, r * capacity, capacity).astype(jnp.bfloat16)
        if r == 0:
            put_halves(outs[0], 0, core, chooser, normed)
            put_halves(outs[1], 0, core, chooser, weighted)
        else:
            put_halves(outs[r + 1], 0, core, chooser, normed)
            put_halves(outs[r + 1], width, core, chooser, weighted)
    pack_ref[:, :width] = act_ref[...]
    pack_ref[:, width : 2 * width] = grad_ref[...]
    lanes = pack_ref.shape[1] - 2 * width
    packed = token_slots(target, experts * capacity, lanes)
    pack_ref[:, 2 * width :] = packed.astype(jnp.float32).astype(jnp.bfloat16)


def join_kernel(*refs):
    *parts, out_ref = refs
    start = 0
    for part in parts:
        out_ref[:, start : start + part.shape[1]] = part[...]
        start += part.shape[1]


def collected(chooser, core, back, capacity, k):
    half = back[0].shape[1] // 2
    start = pl.multiple_of(half * (core if k == 0 else 1 - core), 128)
    columns = pl.ds(start, half)
    first = chooser[:, :capacity]
    total = dot(first, back[0][:, columns]) + dot(first, back[1][:, columns])
    for r, part in enumerate(back[2:], 1):
        total = total + dot(chooser[:, r * capacity : (r + 1) * capacity], part[:, columns])
    return total


def finish_kernel(experts, capacity, pack_ref, *rest):
    *back, out_ref = rest
    core = my_place()[1]
    width = out_ref.shape[1]
    half = width // 2
    slots = experts * capacity
    packed = pack_ref[:, width:]
    parts = packed[:, slots : slots + 3].astype(jnp.float32)
    weight = parts[:, 0:1] + parts[:, 1:2] + parts[:, 2:3]
    for k in range(2):
        columns = slice(k * half, (k + 1) * half)
        mixed = collected(packed, core, back, capacity, k)
        out_ref[:, columns] = (
            pack_ref[:, columns].astype(jnp.float32) + weight * mixed
        ).astype(jnp.bfloat16)


def finish_back_kernel(experts, capacity, pack_ref, *rest):
    *back, out_ref = rest
    core = my_place()[1]
    width = out_ref.shape[1]
    half = width // 2
    packed = pack_ref[:, 2 * width :]
    scaled = [collected(packed, core, back, capacity, k) for k in range(2)]
    widened = [pack_ref[:, k * half : (k + 1) * half].astype(jnp.float32) for k in range(2)]
    squares = sum(jnp.sum(w * w, axis=-1, keepdims=True) for w in widened)
    inverse = lax.rsqrt(squares / width + 1e-06)
    inner = sum(jnp.sum(s * w, axis=-1, keepdims=True) for s, w in zip(scaled, widened))
    factor = inverse * inverse * inverse * (inner / width)
    for k in range(2):
        seed = pack_ref[:, width + k * half : width + (k + 1) * half].astype(jnp.float32)
        out_ref[:, k * half : (k + 1) * half] = (
            seed + scaled[k] * inverse - widened[k] * factor
        ).astype(jnp.bfloat16)


def up_rows(block, half, begin, end):
    large, small, _ = block
    cut = large.shape[0] - half
    return large[half + begin : half + end] if begin < cut else small[begin - cut : end - cut]


def row_ranges(blocks, half):
    cut = max(block[0].shape[0] - half for block in blocks)
    return ((0, cut), (cut, half)) if cut else ((0, half),)


def activations(x_ref, blocks):
    half = x_ref.shape[1] // 2
    pre, upper = 0.0, 0.0
    for k, block in enumerate(blocks):
        first = k * half
        pre = pre + dot(x_ref[:, first : first + half], block[0][:half])
        for begin, end in row_ranges(blocks, half):
            columns = slice(first + begin, first + end)
            upper = upper + dot(x_ref[:, columns], up_rows(block, half, begin, end))
    return pre, upper


def stack_rows(out_ref, pieces):
    width = out_ref.shape[1]
    step = width // 4
    for first in range(0, width, step):
        parts = [ref[:, at + first : at + first + step].astype(jnp.float32) for ref, at in pieces]
        out_ref[:, first : first + step] = jnp.concatenate(parts, axis=0).astype(jnp.bfloat16)


def forward_near_kernel(experts, *refs):
    *near, pair_ref = refs[: experts + 2]
    blocks = refs[experts + 2 : experts + 5], refs[experts + 5 : experts + 8]
    x_ref, part_ref = refs[experts + 8 :]
    pieces = [(ref, 0) for ref in near]
    stack_rows(x_ref, pieces + [(pair_ref, r * x_ref.shape[1]) for r in range(experts - 1)])
    pre, upper = activations(x_ref, blocks)
    hidden = (jax.nn.silu(pre) * upper).astype(jnp.bfloat16)
    half = x_ref.shape[1] // 2
    for k in range(2):
        part_ref[:, k * half : (k + 1) * half] = dot(hidden, blocks[k][2][...])


def put_rows(capacity, total, first, own_ref, near_ref, cross_ref, far_ref):
    columns = slice(first, first + total.shape[1])
    count = total.shape[0] // 2
    own_ref[:, columns] = total[:capacity].astype(jnp.bfloat16)
    far_ref[:, columns] = total[capacity:count]
    near_ref[:, columns] = total[count : count + capacity].astype(jnp.bfloat16)
    cross_ref[:, columns] = total[count + capacity :].astype(jnp.bfloat16)


def forward_side_kernel(capacity, x_ref, part_ref, *refs):
    blocks, outs = (refs[:3], refs[3:6]), refs[6:]
    pre, upper = activations(x_ref, blocks)
    hidden = (jax.nn.silu(pre) * upper).astype(jnp.bfloat16)
    half = x_ref.shape[1] // 2
    for k in range(2):
        total = part_ref[:, k * half : (k + 1) * half] + dot(hidden, blocks[k][2][...])
        put_rows(capacity, total, k * half, *outs)


def backward_kernel(experts, capacity, *refs):
    core = my_place()[1]
    first_ref, grad_ref, *far_refs = refs[: experts + 1]
    pair_ref, rest_ref, gain_ref = refs[experts + 1 : experts + 4]
    blocks = refs[experts + 4 : experts + 16]
    *outs, x_ref, g_ref = refs[experts + 16 :]
    sets = [(blocks[i : i + 3], blocks[i + 3 : i + 6]) for i in (0, 6)]
    width = first_ref.shape[1]
    half = width // 2
    ahead = [(ref, 0) for ref in (first_ref, *far_refs)] + [(pair_ref, pair_ref.shape[1] - width)]
    stack_rows(x_ref, ahead + [(rest_ref, (2 * r - 1) * width) for r in range(1, experts)])
    behind = [(grad_ref, 0)] + [(ref, width) for ref in far_refs] + [(rest_ref, 0)]
    stack_rows(g_ref, behind + [(rest_ref, 2 * r * width) for r in range(1, experts)])
    steps = []
    for blocks in sets:
        pre, upper = activations(x_ref, blocks)
        d_hidden = sum(
            dot_t(g_ref[:, k * half : (k + 1) * half], blocks[k][2][...]) for k in range(2)
        )
        logistic = jax.nn.sigmoid(pre)
        d_gate = d_hidden * upper * logistic * (1.0 + pre * (1.0 - logistic))
        d_up = d_hidden * pre * logistic
        steps.append((d_gate.astype(jnp.bfloat16), d_up.astype(jnp.bfloat16)))
    for k in range(2):
        for begin, end in row_ranges(sets[1], half):
            total = 0.0
            for (d_gate, d_up), blocks in zip(steps, sets):
                upper = up_rows(blocks[k], half, begin, end)
                total = total + dot_t(d_gate, blocks[k][0][begin:end]) + dot_t(d_up, upper)
            start = half * (core if k == 0 else 1 - core) + begin
            gain = gain_ref[:, pl.ds(pl.multiple_of(start, 128), end - begin)]
            put_rows(capacity, gain * total, k * half + begin, *outs)


def send_sums(far, received, experts, capacity, step):
    sums = []
    for r in range(1, experts):
        rows = slice((r - 1) * capacity, r * capacity)
        summed = (far[rows] + received[rows].astype(jnp.float32)).astype(jnp.bfloat16)
        sums.append(to_section(summed, step, lambda i, r=r: i - SLICES * r))
    return sums


def body(
    fwd_act,
    fwd_route,
    fwd_gate,
    bwd_act,
    bwd_grad,
    bwd_route,
    bwd_gate,
    norm_gain,
    w_gate,
    w_up,
    w_down,
):
    experts = lax.axis_size("ep") // SLICES
    tokens, width = fwd_act.shape[1:]
    capacity = 2 * ((5 * tokens + 8 * experts - 1) // (8 * experts))
    shifts = range(1, experts)
    gate, up, down = w_gate[0, 0], w_up[0, 0], w_down[0, 0]
    row = (1, tokens)
    lanes = -(-(experts * capacity + 3) // 128) * 128
    slots = ((capacity, width), jnp.bfloat16)
    two_slots = ((capacity, 2 * width), jnp.bfloat16)

    large, small = split_weights(gate, up)
    side_down = swap(down, SIDE)
    fwd_pack, *fwd_groups = call_fetching(
        functools.partial(prepare_kernel, experts, capacity),
        "prepare",
        [((tokens, width + lanes), jnp.bfloat16)] + [slots] * experts,
        LONG,
        (fwd_route.reshape(row), fwd_gate.reshape(row), fwd_act[0], norm_gain),
    )
    fwd_far = [to_expert(fwd_groups[r], r) for r in shifts]
    first_pair = swap(fwd_groups[0], FAR)
    near_down = swap(after(down, fwd_groups[0]), NEAR)
    fwd_pack = to_section(fwd_pack, 1)
    bwd_pack, bwd_first, grad_first, *bwd_groups = call(
        functools.partial(prepare_back_kernel, experts, capacity),
        "prepare_back",
        [((tokens, 2 * width + lanes), jnp.bfloat16), slots, slots] + [two_slots] * (experts - 1),
        SHORT,
        (bwd_route.reshape(row), bwd_gate.reshape(row), bwd_act[0], bwd_grad[0], norm_gain),
        held=8,
    )

    first = (side_down, near_down, fwd_pack, first_pair, bwd_first, large, *fwd_far)
    bwd_pack = to_section(after(bwd_pack, *first), -1)
    near_up = swap(after(up, *first), NEAR)
    (mixed,) = call(
        join_kernel,
        "join",
        [((capacity, experts * width), jnp.bfloat16)],
        SHORT,
        (*after(tuple(fwd_far), *first), bwd_first),
    )
    own_pair = swap(mixed, FAR)
    side_large = swap(after(large, *first), SIDE)
    bwd_far = [to_expert(after(bwd_groups[r - 1], *first), r) for r in shifts]

    (rest,) = call(
        join_kernel,
        "join_back",
        [((capacity, (2 * experts - 1) * width), jnp.bfloat16)],
        LONG,
        (after(grad_first, side_large), *bwd_far),
    )
    second = (rest, bwd_pack, near_up, own_pair)
    rest_pair = swap(rest, FAR)
    near_gate = swap(after(gate, *second), NEAR)
    side_small = swap(after(small, *second), SIDE)
    side_near_large = swap(after(side_large, *second), NEAR)
    side_near_down = swap(after(side_down, *second), NEAR)
    mine = ((gate, up, down), (near_gate, near_up, near_down))

    rows = (2 * experts * capacity, width)
    far = ((experts - 1) * capacity, width)
    outs = [slots, slots, (far, jnp.bfloat16), (far, jnp.float32)]
    pieces = after((fwd_groups[0], *fwd_far, first_pair, own_pair), rest, side_near_down)
    fwd_x, part = call(
        functools.partial(forward_near_kernel, experts),
        "forward_near",
        [(rows, jnp.bfloat16), (rows, jnp.float32)],
        SHORT,
        (*pieces, *mine[0], *mine[1]),
        held=6,
    )
    side_near_small = swap(after(side_small, part, side_near_large), NEAR)
    beside = ((side_large, side_small, side_down), (side_near_large, side_near_small, side_near_down))
    fwd_own, fwd_near, fwd_cross, fwd_sum = call(
        functools.partial(forward_side_kernel, capacity),
        "forward_side",
        outs,
        SHORT,
        (fwd_x, part, *beside[0], *beside[1]),
        held=6,
    )
    rest_pair = after(rest_pair, fwd_own)
    fwd_received = swap(fwd_cross, FAR)
    fwd_second = to_section(fwd_near, 1, lambda i: i ^ FAR)
    fwd_near_sums = to_section(fwd_own, 1)

    bwd_own, bwd_near, bwd_cross, bwd_sum = call(
        functools.partial(backward_kernel, experts, capacity),
        "backward",
        outs,
        SHORT,
        (bwd_first, grad_first, *bwd_far, own_pair, rest_pair, norm_gain)
        + (*mine[0], *mine[1], *beside[0], *beside[1]),
        held=14,
        scratch=(pltpu.VMEM(rows, jnp.bfloat16),) * 2,
    )
    bwd_received = swap(after(bwd_cross, fwd_received), FAR)
    fwd_sums = send_sums(fwd_sum, fwd_received, experts, capacity, 1)
    bwd_near_sums = to_section(after(bwd_own, fwd_received), -1)
    bwd_sums = send_sums(bwd_sum, bwd_received, experts, capacity, -1)
    both = (fwd_received, bwd_received)
    bwd_second = to_section(after(bwd_near, *both), -1, lambda i: i ^ FAR)
    fwd_back = (fwd_near_sums, fwd_second, *fwd_sums)
    bwd_back = (bwd_near_sums, bwd_second, *bwd_sums)

    (fwd_next,) = call(
        functools.partial(finish_kernel, experts, capacity),
        "finish",
        [((tokens, width), jnp.bfloat16)],
        SHORT,
        (fwd_pack, *fwd_back),
        held=8,
    )
    (held_pack,) = call(
        join_kernel,
        "hold",
        [(bwd_pack.shape, jnp.bfloat16)],
        SHORT,
        (after(bwd_pack, bwd_received),),
    )
    (bwd_next,) = call(
        functools.partial(finish_back_kernel, experts, capacity),
        "finish_back",
        [((tokens, width), jnp.bfloat16)],
        SHORT,
        (held_pack, *bwd_back),
        held=8,
    )
    return (fwd_next[None], bwd_next[None])


def solution(mesh):
    rows = P("pp", "ep", None)
    weights = P("pp", "ep", None, None)
    in_specs = (rows,) * 7 + (P("pp", None),) + (weights,) * 3
    return jax.shard_map(
        body, mesh=mesh, in_specs=in_specs, out_specs=(rows, rows), check_vma=False
    )
```

```python
import functools

import jax
import jax.numpy as jnp
from jax import lax
from jax.experimental import pallas as pl
from jax.experimental.pallas import tpu as pltpu
from jax.sharding import PartitionSpec as P

SLICES = 8
NEAR, SIDE, FAR = 1, 2, 4
SHORT, LONG = 10**6, 2 * 10**11
FULL = 58 * 2**20


def swap(value, bit):
    return lax.ppermute(value, "ep", [(i, i ^ bit) for i in range(lax.axis_size("ep"))])


def to_expert(value, shift):
    count = lax.axis_size("ep")
    return lax.ppermute(value, "ep", [(i, (i + SLICES * shift) % count) for i in range(count)])


def to_section(value, step, place=lambda i: i):
    sections, count = lax.axis_size("pp"), lax.axis_size("ep")
    pairs = [
        (p * count + i, (p + step) % sections * count + place(i) % count)
        for p in range(sections)
        for i in range(count)
    ]
    return lax.ppermute(value, ("pp", "ep"), pairs)


def after(value, *done):
    return lax.optimization_barrier((value, done))[0]


def dot(a, b):
    return jnp.dot(a, b, preferred_element_type=jnp.float32)


def dot_t(a, b):
    return lax.dot_general(a, b, (((1,), (1,)), ((), ())), preferred_element_type=jnp.float32)


def dot_first(a, b):
    return lax.dot_general(a, b, (((0,), (0,)), ((), ())), preferred_element_type=jnp.float32)


def call(kernel, name, outs, cost, args, held=1, scratch=()):
    space = pl.BlockSpec(memory_space=pltpu.VMEM)
    return pl.pallas_call(
        kernel,
        name=name,
        out_shape=[jax.ShapeDtypeStruct(shape, kind) for shape, kind in outs],
        in_specs=[space] * len(args),
        out_specs=[space] * len(outs),
        scratch_shapes=list(scratch),
        cost_estimate=pl.CostEstimate(flops=cost, bytes_accessed=0, transcendentals=0),
        compiler_params=pltpu.CompilerParams(vmem_limit_bytes=held * 2**20),
    )(*args)


def call_fetching(kernel, name, outs, cost, args):
    count = len(args)

    def fetching(*refs):
        sources, rest = refs[:count], refs[count : count + len(outs)]
        held, sems = refs[count + len(outs) : -1], refs[-1]
        copies = [
            pltpu.make_async_copy(source, target, sems.at[i])
            for i, (source, target) in enumerate(zip(sources, held))
        ]
        for copy in copies:
            copy.start()
        for copy in copies:
            copy.wait()
        kernel(*held, *rest)

    return pl.pallas_call(
        fetching,
        name=name,
        out_shape=[jax.ShapeDtypeStruct(shape, kind) for shape, kind in outs],
        in_specs=[pl.BlockSpec(memory_space=pltpu.HBM)] * count,
        out_specs=[pl.BlockSpec(memory_space=pltpu.VMEM)] * len(outs),
        scratch_shapes=[pltpu.VMEM(arg.shape, arg.dtype) for arg in args]
        + [pltpu.SemaphoreType.DMA((count,))],
        cost_estimate=pl.CostEstimate(flops=cost, bytes_accessed=0, transcendentals=0),
        compiler_params=pltpu.CompilerParams(vmem_limit_bytes=FULL),
    )(*args)


def my_place():
    me = lax.axis_index("ep")
    return me // SLICES, me % 2


def split_kernel(gate_ref, up_ref, large_ref, small_ref, sems):
    half, cut = gate_ref.shape[0], up_ref.shape[0] - small_ref.shape[0]
    copies = [
        pltpu.make_async_copy(gate_ref, large_ref.at[pl.ds(0, half)], sems.at[0]),
        pltpu.make_async_copy(up_ref.at[pl.ds(0, cut)], large_ref.at[pl.ds(half, cut)], sems.at[1]),
        pltpu.make_async_copy(up_ref.at[pl.ds(cut, half - cut)], small_ref, sems.at[2]),
    ]
    for copy in copies:
        copy.start()
    for copy in copies:
        copy.wait()


def split_weights(gate, up):
    half, units = up.shape
    cut = half * 3 // 7 // 128 * 128
    anywhere = pl.BlockSpec(memory_space=pl.ANY)
    return pl.pallas_call(
        split_kernel,
        name="split_weights",
        out_shape=[
            jax.ShapeDtypeStruct((half + cut, units), up.dtype),
            jax.ShapeDtypeStruct((half - cut, units), up.dtype),
        ],
        in_specs=[anywhere] * 2,
        out_specs=[anywhere] * 2,
        scratch_shapes=[pltpu.SemaphoreType.DMA((3,))],
        cost_estimate=pl.CostEstimate(flops=SHORT, bytes_accessed=0, transcendentals=0),
        compiler_params=pltpu.CompilerParams(vmem_limit_bytes=2 * 2**20),
    )(gate, up)


def slot_rows(route_ref, mine, experts, capacity):
    chosen = route_ref[...]
    tokens = chosen.shape[1]
    onehot = lax.broadcasted_iota(jnp.int32, (experts, tokens), 0) == chosen
    before = lax.broadcasted_iota(jnp.int32, (tokens, tokens), 0) <= lax.broadcasted_iota(
        jnp.int32, (tokens, tokens), 1
    )
    running = dot(onehot.astype(jnp.bfloat16), before.astype(jnp.bfloat16))
    position = jnp.sum(jnp.where(onehot, running, 0.0), axis=0, keepdims=True) - 1.0
    relative = chosen - mine
    relative = jnp.where(relative < 0, relative + experts, relative)
    return relative * capacity + position.astype(jnp.int32)


def choose(target, first, count):
    slots = lax.broadcasted_iota(jnp.int32, (count, target.shape[1]), 0)
    return slots == target - first


def to_column(row):
    size = row.shape[1]
    same = lax.broadcasted_iota(jnp.int32, (size, size), 0) == lax.broadcasted_iota(
        jnp.int32, (size, size), 1
    )
    return jnp.sum(jnp.where(same, row, 0.0), axis=1, keepdims=True)


def inverse_rms(widened):
    return lax.rsqrt(jnp.mean(widened * widened, axis=-1, keepdims=True) + 1e-06)


def put_halves(out_ref, first, core, chooser, rows):
    half = rows.shape[1] // 2
    for k in range(2):
        placed = dot(chooser, rows[:, k * half : (k + 1) * half]).astype(jnp.bfloat16)
        start = first + half * (core if k == 0 else 1 - core)
        out_ref[:, pl.ds(pl.multiple_of(start, 128), half)] = placed


def token_slots(target, count, lanes):
    column = to_column(target.astype(jnp.float32)).astype(jnp.int32)
    return lax.broadcasted_iota(jnp.int32, (target.shape[1], lanes), 1) == column


def prepare_kernel(experts, capacity, route_ref, gate_ref, act_ref, gain_ref, pack_ref, *outs):
    mine, core = my_place()
    width = act_ref.shape[1]
    target = slot_rows(route_ref, mine, experts, capacity)
    widened = act_ref[...].astype(jnp.float32)
    normed = (widened * inverse_rms(widened) * gain_ref[...]).astype(jnp.bfloat16)
    for r in range(experts):
        chooser = choose(target, r * capacity, capacity).astype(jnp.bfloat16)
        put_halves(outs[r], 0, core, chooser, normed)
    pack_ref[:, :width] = act_ref[...]
    lanes = pack_ref.shape[1] - width
    slots = experts * capacity
    packed = token_slots(target, slots, lanes).astype(jnp.float32)
    rest = to_column(gate_ref[...])
    lane = lax.broadcasted_iota(jnp.int32, packed.shape, 1)
    for part in range(3):
        piece = rest.astype(jnp.bfloat16).astype(jnp.float32)
        packed = jnp.where(lane == slots + part, piece, packed)
        rest = rest - piece
    pack_ref[:, width:] = packed.astype(jnp.bfloat16)


def prepare_back_kernel(
    experts, capacity, route_ref, gate_ref, act_ref, grad_ref, gain_ref, pack_ref, *outs
):
    mine, core = my_place()
    width = act_ref.shape[1]
    target = slot_rows(route_ref, mine, experts, capacity)
    widened = act_ref[...].astype(jnp.float32)
    normed = (widened * inverse_rms(widened) * gain_ref[...]).astype(jnp.bfloat16)
    weighted = (to_column(gate_ref[...]) * grad_ref[...].astype(jnp.float32)).astype(jnp.bfloat16)
    for r in range(experts):
        chooser = choose(target, r * capacity, capacity).astype(jnp.bfloat16)
        if r == 0:
            put_halves(outs[0], 0, core, chooser, normed)
            put_halves(outs[1], 0, core, chooser, weighted)
        else:
            put_halves(outs[r + 1], 0, core, chooser, normed)
            put_halves(outs[r + 1], width, core, chooser, weighted)
    pack_ref[:, :width] = act_ref[...]
    pack_ref[:, width : 2 * width] = grad_ref[...]
    lanes = pack_ref.shape[1] - 2 * width
    packed = token_slots(target, experts * capacity, lanes)
    pack_ref[:, 2 * width :] = packed.astype(jnp.float32).astype(jnp.bfloat16)


def join_kernel(*refs):
    *parts, out_ref = refs
    start = 0
    for part in parts:
        out_ref[:, start : start + part.shape[1]] = part[...]
        start += part.shape[1]


def collected(chooser, core, back, capacity, k):
    half = back[0].shape[1] // 2
    start = pl.multiple_of(half * (core if k == 0 else 1 - core), 128)
    columns = pl.ds(start, half)
    first = chooser[:, :capacity]
    total = dot(first, back[0][:, columns]) + dot(first, back[1][:, columns])
    for r, part in enumerate(back[2:], 1):
        total = total + dot(chooser[:, r * capacity : (r + 1) * capacity], part[:, columns])
    return total


def finish_kernel(experts, capacity, pack_ref, *rest):
    *back, out_ref = rest
    core = my_place()[1]
    width = out_ref.shape[1]
    half = width // 2
    slots = experts * capacity
    packed = pack_ref[:, width:]
    parts = packed[:, slots : slots + 3].astype(jnp.float32)
    weight = parts[:, 0:1] + parts[:, 1:2] + parts[:, 2:3]
    for k in range(2):
        columns = slice(k * half, (k + 1) * half)
        mixed = collected(packed, core, back, capacity, k)
        out_ref[:, columns] = (
            pack_ref[:, columns].astype(jnp.float32) + weight * mixed
        ).astype(jnp.bfloat16)


def finish_back_kernel(experts, capacity, pack_ref, *rest):
    *back, out_ref = rest
    core = my_place()[1]
    width = out_ref.shape[1]
    half = width // 2
    packed = pack_ref[:, 2 * width :]
    scaled = [collected(packed, core, back, capacity, k) for k in range(2)]
    widened = [pack_ref[:, k * half : (k + 1) * half].astype(jnp.float32) for k in range(2)]
    squares = sum(jnp.sum(w * w, axis=-1, keepdims=True) for w in widened)
    inverse = lax.rsqrt(squares / width + 1e-06)
    inner = sum(jnp.sum(s * w, axis=-1, keepdims=True) for s, w in zip(scaled, widened))
    factor = inverse * inverse * inverse * (inner / width)
    for k in range(2):
        seed = pack_ref[:, width + k * half : width + (k + 1) * half].astype(jnp.float32)
        out_ref[:, k * half : (k + 1) * half] = (
            seed + scaled[k] * inverse - widened[k] * factor
        ).astype(jnp.bfloat16)


def up_rows(block, half, begin, end):
    large, small, _ = block
    cut = large.shape[0] - half
    return large[half + begin : half + end] if begin < cut else small[begin - cut : end - cut]


def row_ranges(blocks, half):
    cut = max(block[0].shape[0] - half for block in blocks)
    return ((0, cut), (cut, half)) if cut else ((0, half),)


def activations(x_ref, blocks):
    half = x_ref.shape[1] // 2
    pre, upper = 0.0, 0.0
    for k, block in enumerate(blocks):
        first = k * half
        pre = pre + dot(x_ref[:, first : first + half], block[0][:half])
        for begin, end in row_ranges(blocks, half):
            columns = slice(first + begin, first + end)
            upper = upper + dot(x_ref[:, columns], up_rows(block, half, begin, end))
    return pre, upper


def stack_rows(out_ref, pieces):
    width = out_ref.shape[1]
    step = width // 4
    for first in range(0, width, step):
        parts = [ref[:, at + first : at + first + step].astype(jnp.float32) for ref, at in pieces]
        out_ref[:, first : first + step] = jnp.concatenate(parts, axis=0).astype(jnp.bfloat16)


def forward_near_kernel(experts, *refs):
    *near, pair_ref = refs[: experts + 2]
    blocks = refs[experts + 2 : experts + 5], refs[experts + 5 : experts + 8]
    x_ref, part_ref = refs[experts + 8 :]
    pieces = [(ref, 0) for ref in near]
    stack_rows(x_ref, pieces + [(pair_ref, r * x_ref.shape[1]) for r in range(experts - 1)])
    pre, upper = activations(x_ref, blocks)
    hidden = (jax.nn.silu(pre) * upper).astype(jnp.bfloat16)
    half = x_ref.shape[1] // 2
    for k in range(2):
        part_ref[:, k * half : (k + 1) * half] = dot(hidden, blocks[k][2][...])


def put_rows(capacity, total, first, own_ref, near_ref, cross_ref, far_ref):
    columns = slice(first, first + total.shape[1])
    count = total.shape[0] // 2
    own_ref[:, columns] = total[:capacity].astype(jnp.bfloat16)
    far_ref[:, columns] = total[capacity:count]
    near_ref[:, columns] = total[count : count + capacity].astype(jnp.bfloat16)
    cross_ref[:, columns] = total[count + capacity :].astype(jnp.bfloat16)


def forward_side_kernel(capacity, x_ref, part_ref, *refs):
    blocks, outs = (refs[:3], refs[3:6]), refs[6:]
    pre, upper = activations(x_ref, blocks)
    hidden = (jax.nn.silu(pre) * upper).astype(jnp.bfloat16)
    half = x_ref.shape[1] // 2
    for k in range(2):
        total = part_ref[:, k * half : (k + 1) * half] + dot(hidden, blocks[k][2][...])
        put_rows(capacity, total, k * half, *outs)


def backward_kernel(experts, capacity, *refs):
    core = my_place()[1]
    first_ref, grad_ref, *far_refs = refs[: experts + 1]
    pair_ref, rest_ref, gain_ref = refs[experts + 1 : experts + 4]
    blocks = refs[experts + 4 : experts + 16]
    *outs, x_ref, g_ref = refs[experts + 16 :]
    sets = [(blocks[i : i + 3], blocks[i + 3 : i + 6]) for i in (0, 6)]
    width = first_ref.shape[1]
    half = width // 2
    ahead = [(ref, 0) for ref in (first_ref, *far_refs)] + [(pair_ref, pair_ref.shape[1] - width)]
    stack_rows(x_ref, ahead + [(rest_ref, (2 * r - 1) * width) for r in range(1, experts)])
    behind = [(grad_ref, 0)] + [(ref, width) for ref in far_refs] + [(rest_ref, 0)]
    stack_rows(g_ref, behind + [(rest_ref, 2 * r * width) for r in range(1, experts)])
    steps = []
    for blocks in sets:
        pre, upper = activations(x_ref, blocks)
        d_hidden = sum(
            dot_t(g_ref[:, k * half : (k + 1) * half], blocks[k][2][...]) for k in range(2)
        )
        logistic = jax.nn.sigmoid(pre)
        d_gate = d_hidden * upper * logistic * (1.0 + pre * (1.0 - logistic))
        d_up = d_hidden * pre * logistic
        steps.append((d_gate.astype(jnp.bfloat16), d_up.astype(jnp.bfloat16)))
    for k in range(2):
        for begin, end in row_ranges(sets[1], half):
            total = 0.0
            for (d_gate, d_up), blocks in zip(steps, sets):
                upper = up_rows(blocks[k], half, begin, end)
                total = total + dot_t(d_gate, blocks[k][0][begin:end]) + dot_t(d_up, upper)
            start = half * (core if k == 0 else 1 - core) + begin
            gain = gain_ref[:, pl.ds(pl.multiple_of(start, 128), end - begin)]
            put_rows(capacity, gain * total, k * half + begin, *outs)


def add_rows(kept, received, count, capacity):
    return [
        (kept[rows] + received[rows].astype(jnp.float32)).astype(jnp.bfloat16)
        for rows in (slice(i * capacity, (i + 1) * capacity) for i in range(count))
    ]


def send_sums(sums, step):
    return [
        to_section(part, step, lambda i, r=r: i - SLICES * r) for r, part in enumerate(sums, 1)
    ]


def body(
    fwd_act,
    fwd_route,
    fwd_gate,
    bwd_act,
    bwd_grad,
    bwd_route,
    bwd_gate,
    norm_gain,
    w_gate,
    w_up,
    w_down,
):
    experts = lax.axis_size("ep") // SLICES
    tokens, width = fwd_act.shape[1:]
    capacity = 2 * ((5 * tokens + 8 * experts - 1) // (8 * experts))
    shifts = range(1, experts)
    gate, up, down = w_gate[0, 0], w_up[0, 0], w_down[0, 0]
    row = (1, tokens)
    lanes = -(-(experts * capacity + 3) // 128) * 128
    slots = ((capacity, width), jnp.bfloat16)
    two_slots = ((capacity, 2 * width), jnp.bfloat16)

    large, small = split_weights(gate, up)
    side_down = swap(down, SIDE)
    fwd_pack, *fwd_groups = call_fetching(
        functools.partial(prepare_kernel, experts, capacity),
        "prepare",
        [((tokens, width + lanes), jnp.bfloat16)] + [slots] * experts,
        LONG,
        (fwd_route.reshape(row), fwd_gate.reshape(row), fwd_act[0], norm_gain),
    )
    fwd_far = [to_expert(fwd_groups[r], r) for r in shifts]
    first_pair = swap(fwd_groups[0], FAR)
    near_down = swap(after(down, fwd_groups[0]), NEAR)
    fwd_pack = to_section(fwd_pack, 1)
    bwd_pack, bwd_first, grad_first, *bwd_groups = call(
        functools.partial(prepare_back_kernel, experts, capacity),
        "prepare_back",
        [((tokens, 2 * width + lanes), jnp.bfloat16), slots, slots] + [two_slots] * (experts - 1),
        SHORT,
        (bwd_route.reshape(row), bwd_gate.reshape(row), bwd_act[0], bwd_grad[0], norm_gain),
        held=8,
    )

    first = (side_down, near_down, fwd_pack, first_pair, bwd_first, large, *fwd_far)
    bwd_pack = to_section(after(bwd_pack, *first), -1)
    near_up = swap(after(up, *first), NEAR)
    (mixed,) = call(
        join_kernel,
        "join",
        [((capacity, experts * width), jnp.bfloat16)],
        SHORT,
        (*after(tuple(fwd_far), *first), bwd_first),
    )
    own_pair = swap(mixed, FAR)
    side_large = swap(after(large, *first), SIDE)
    bwd_far = [to_expert(after(bwd_groups[r - 1], *first), r) for r in shifts]

    (rest,) = call(
        join_kernel,
        "join_back",
        [((capacity, (2 * experts - 1) * width), jnp.bfloat16)],
        LONG,
        (after(grad_first, side_large), *bwd_far),
    )
    second = (rest, bwd_pack, near_up, own_pair)
    rest_pair = swap(rest, FAR)
    near_gate = swap(after(gate, *second), NEAR)
    side_small = swap(after(small, *second), SIDE)
    side_near_large = swap(after(side_large, *second), NEAR)
    side_near_down = swap(after(side_down, *second), NEAR)
    mine = ((gate, up, down), (near_gate, near_up, near_down))

    rows = (2 * experts * capacity, width)
    far = ((experts - 1) * capacity, width)
    outs = [slots, slots, (far, jnp.bfloat16), (far, jnp.float32)]
    pieces = after((fwd_groups[0], *fwd_far, first_pair, own_pair), rest, side_near_down)
    fwd_x, part = call(
        functools.partial(forward_near_kernel, experts),
        "forward_near",
        [(rows, jnp.bfloat16), (rows, jnp.float32)],
        SHORT,
        (*pieces, *mine[0], *mine[1]),
        held=6,
    )
    side_near_small = swap(after(side_small, part, side_near_large), NEAR)
    beside = ((side_large, side_small, side_down), (side_near_large, side_near_small, side_near_down))
    fwd_own, fwd_near, fwd_cross, fwd_sum = call(
        functools.partial(forward_side_kernel, capacity),
        "forward_side",
        outs,
        SHORT,
        (fwd_x, part, *beside[0], *beside[1]),
        held=6,
    )
    rest_pair = after(rest_pair, fwd_own)
    fwd_received = swap(fwd_cross, FAR)
    fwd_second = to_section(fwd_near, 1, lambda i: i ^ FAR)
    fwd_near_sums = to_section(fwd_own, 1)

    bwd_own, bwd_near, bwd_cross, bwd_sum = call(
        functools.partial(backward_kernel, experts, capacity),
        "backward",
        outs,
        SHORT,
        (bwd_first, grad_first, *bwd_far, own_pair, rest_pair, norm_gain)
        + (*mine[0], *mine[1], *beside[0], *beside[1]),
        held=14,
        scratch=(pltpu.VMEM(rows, jnp.bfloat16),) * 2,
    )
    bwd_received = swap(after(bwd_cross, fwd_received), FAR)
    fwd_sums = send_sums(add_rows(fwd_sum, fwd_received, experts - 1, capacity), 1)
    bwd_near_sums = to_section(after(bwd_own, fwd_received), -1)
    bwd_totals = add_rows(bwd_sum, bwd_received, experts - 1, capacity)
    bwd_sums = send_sums(bwd_totals, -1)
    both = (fwd_received, bwd_received)
    bwd_second = to_section(after(bwd_near, *both, *bwd_totals), -1, lambda i: i ^ FAR)
    fwd_back = (fwd_near_sums, fwd_second, *fwd_sums)
    bwd_back = (bwd_near_sums, bwd_second, *bwd_sums)

    (fwd_next,) = call(
        functools.partial(finish_kernel, experts, capacity),
        "finish",
        [((tokens, width), jnp.bfloat16)],
        SHORT,
        (fwd_pack, *fwd_back),
        held=8,
    )
    (held_pack,) = call(
        join_kernel,
        "hold",
        [(bwd_pack.shape, jnp.bfloat16)],
        SHORT,
        (after(bwd_pack, bwd_received),),
    )
    (bwd_next,) = call(
        functools.partial(finish_back_kernel, experts, capacity),
        "finish_back",
        [((tokens, width), jnp.bfloat16)],
        SHORT,
        (held_pack, *bwd_back),
        held=8,
    )
    return (fwd_next[None], bwd_next[None])


def solution(mesh):
    rows = P("pp", "ep", None)
    weights = P("pp", "ep", None, None)
    in_specs = (rows,) * 7 + (P("pp", None),) + (weights,) * 3
    return jax.shard_map(
        body, mesh=mesh, in_specs=in_specs, out_specs=(rows, rows), check_vma=False
    )
```
